256 devices in a mesh: space: 32 (over x_hi, z, core), tensor: 8 (over y, x_lo).
Axes of the slice: x: 4 (x_hi: 2, x_lo: 2; x = x_hi * 2 + x_lo), y: 4, z: 8, core: 2. Of those that a mesh axis runs over, the one named last changes fastest.
Arguments:
- field: bfloat16 [32, 32, 8192], P('space', None, 'tensor'), may hold values from -6 to 6
- w_in: bfloat16 [8192, 28672], P('tensor', 'space'), may hold values from -0.0625 to 0.0625
- w_out: bfloat16 [28672, 8192], P('space', 'tensor'), may hold values from -0.03125 to 0.03125
- kernel: float32 [9, 8192], P(None, 'tensor'), may hold values from -1.5 to 1.5
- cotangent: bfloat16 [32, 32, 8192], P('space', None, 'tensor'), may hold values from -6 to 6
Outputs:
- result: float32 [32, 32, 8192], P('space', None, 'tensor')
- field_grad: float32 [32, 32, 8192], P('space', None, 'tensor')
- grad_in: float32 [8192, 28672], P('tensor', 'space')
- grad_out: float32 [28672, 8192], P('space', 'tensor')
- grad_kernel: float32 [9, 8192], P(None, 'tensor')
The draws below stay inside these ranges and needn't reach their ends.
All inputs are finite; a program needn't handle non-finite values.
Results may differ from the reference program's by a relative error of at most 0.029.
Values may be sent and summed in bfloat16 or wider, within the bound.
A program may use at most 128 MiB of HBM per device.

```python
import math
import jax
import jax.numpy as jnp
from jax import lax

D = 8192
FF = 28672
COLS = 32
GRID_ROWS = 32
TOKENS = 1024
N_SPACE = 32
N_TENSOR = 8


def block_scale(own_key, shape, split, least, largest):
    def one(axis_at, shards_of):
        draws = jax.random.uniform(jax.random.fold_in(jax.random.fold_in(own_key, 6), axis_at), (shards_of,), jnp.float32, least / len(split), largest / len(split))
        return jnp.repeat(jnp.exp(draws), shape[axis_at] // shards_of).reshape((-1,) + (1,) * (len(shape) - axis_at - 1))

    gain = one(*split[0])
    for cut in split[1:]:
        gain = gain * one(*cut)
    return gain


def scatter_about(own_key, dims, scale, limit, cuts=(), kind=jnp.bfloat16):
    drawn = scale * jax.random.normal(own_key, dims, jnp.float32)
    if cuts:
        drawn = drawn * block_scale(own_key, dims, cuts, -0.22, 0.18)
    return jnp.clip(drawn, -limit, limit).astype(kind)


def setup_inputs(seed: int = 0) -> dict:
    key_list = jax.random.split(jax.random.key(seed), 6)
    return {
        "field": scatter_about(key_list[0], (GRID_ROWS, COLS, D), 1.0, 6.0, ((0, 32), (2, 8))),
        "w_in": scatter_about(key_list[1], (D, FF), D ** -0.5, 0.0625, ((0, 8), (1, 32))),
        "w_out": scatter_about(key_list[2], (FF, D), FF ** -0.5, 0.03125, ((0, 32), (1, 8))),
        "kernel": scatter_about(key_list[3], (9, D), 0.3, 1.5, ((1, 8),), jnp.float32),
        "cotangent": scatter_about(key_list[4], (GRID_ROWS, COLS, D), 1.0, 6.0, ((0, 32), (2, 8))),
    }


OFFSETS = [(-1, -1), (-1, 0), (-1, 1), (0, -1), (0, 0), (0, 1), (1, -1), (1, 0), (1, 1)]

def rounded_sum(left, right, blocks):
    width = left.shape[1] // blocks

    def step(total, index):
        first = (index * width).astype(jnp.int32)
        left_part = lax.dynamic_slice_in_dim(left, first, width, 1)
        right_part = lax.dynamic_slice_in_dim(right, first, width, 0)
        partial_value = jnp.dot(left_part, right_part, preferred_element_type=jnp.float32).astype(jnp.bfloat16)
        partial_value = lax.optimization_barrier(partial_value)
        return (total + partial_value.astype(jnp.float32), None)
    start_total = jnp.zeros((left.shape[0], right.shape[1]), jnp.float32)
    total, _ = lax.scan(step, start_total, jnp.arange(blocks, dtype=jnp.int32))
    return total

def reference(field, w_in, w_out, kernel, cotangent):
    factor = 1.0 / math.sqrt(TOKENS)
    taps = kernel.astype(jnp.float32)
    field_f32 = field.astype(jnp.float32)
    spread = jnp.zeros(field.shape, jnp.float32)
    for tap_index, (row_step, col_step) in enumerate(OFFSETS):
        spread = spread + taps[tap_index] * jnp.roll(field_f32, (-row_step, -col_step), axis=(0, 1))
    mixed = (field_f32 + spread).astype(jnp.bfloat16)
    flat_mixed = mixed.reshape(-1, D)
    hidden = rounded_sum(flat_mixed, w_in, N_TENSOR)
    activ, gelu_back = jax.vjp(jax.nn.gelu, hidden)
    activation = activ.astype(jnp.bfloat16)
    result = rounded_sum(activation, w_out, N_SPACE).reshape(GRID_ROWS, COLS, D)
    flat_grad = cotangent.reshape(-1, D)
    grad_out = jnp.dot(activation.T, flat_grad, preferred_element_type=jnp.float32) * factor
    act_grad = rounded_sum(flat_grad, w_out.T, N_TENSOR)
    hidden_grad = gelu_back(act_grad)[0].astype(jnp.bfloat16)
    grad_in = jnp.dot(flat_mixed.T, hidden_grad, preferred_element_type=jnp.float32) * factor
    mixed_grad = rounded_sum(hidden_grad, w_in.T, N_SPACE).reshape(GRID_ROWS, COLS, D)
    field_grad = mixed_grad
    kernel_rows = []
    for tap_index, (row_step, col_step) in enumerate(OFFSETS):
        field_grad = field_grad + taps[tap_index] * jnp.roll(mixed_grad, (row_step, col_step), axis=(0, 1))
        moved = jnp.roll(field_f32, (-row_step, -col_step), axis=(0, 1))
        kernel_rows.append(lax.optimization_barrier(jnp.sum(mixed_grad * moved, axis=(0, 1))))
    grad_kernel = jnp.stack(kernel_rows, axis=0) * factor
    return (result, field_grad, grad_in, grad_out, grad_kernel)
```

```python
import functools
import math

import jax
import jax.numpy as jnp
from jax import lax
from jax.experimental import pallas as pl
from jax.experimental.pallas import tpu as pltpu
from jax.sharding import PartitionSpec as P

MESH = pl.DeviceIdType.MESH
F32, BF16 = jnp.float32, jnp.bfloat16
OFFSETS = [(-1, -1), (-1, 0), (-1, 1), (0, -1), (0, 0), (0, 1), (1, -1), (1, 0), (1, 1)]

NZ, NY, NT = 8, 4, 8
COLS, TOKENS, DB, FB = 32, 1024, 1024, 896
FACTOR = 1.0 / math.sqrt(TOKENS)

ORDER = [0, 1, 7, 2, 6, 3, 5, 4]
POS = {dz: 128 * i for i, dz in enumerate(ORDER)}
CHUNKS = [(0, 128), (128, 256), (384, 256), (640, 256), (896, 128)]
CHUNK_DZ = [[0], [1, 7], [2, 6], [3, 5], [4]]
OWN = [0, 16, 48, 80, 112]
RELS = [(dy, dx) for dy in range(NY) for dx in range(2) if (dy, dx) != (0, 0)]


def gelu_pair(hidden):
    c = math.sqrt(2.0 / math.pi)
    square = hidden * hidden
    th = jnp.tanh(c * (hidden + 0.044715 * (square * hidden)))
    half = 0.5 * (1.0 + th)
    slope = half + 0.5 * hidden * (1.0 - th * th) * (c * (1.0 + (3.0 * 0.044715) * square))
    return hidden * half, slope


def kernel(
    field_ref, cot_ref, taps_ref, wi_hbm, wo_hbm,
    result_ref, fgrad_ref, kgrad_ref, a_hbm, hg_hbm, mx_hbm, ct_hbm,
    wi, wo, ct, mx, gp, hp, rg, rh, own_g, av, hv,
    pm, pr, sbm, sbr, qm, qr, rrm, rrr, xrm, xrr, halo, mg, mhalo,
    kp, kr, kz, kf, kg,
    lsem, halo_s, halo_r, ag_s, ag_r, sib_r, rs_s, rs_r, at_s, at_r,
    sc_s, sc_sib, sc_ring, sc_x, mh_s, mh_r, k_s, k_r,
):
    s, t = lax.axis_index("space"), lax.axis_index("tensor")
    core, z, xh = s % 2, (s // 2) % NZ, s // (2 * NZ)
    y, xl = t // 2, t % 2

    def zdev(dz):
        return ((xh * NZ + (z + dz) % NZ) * 2 + core, t)

    def tdev(rel):
        return (s, ((y + rel[0]) % NY) * 2 + (xl + rel[1]) % 2)

    xdev = (((1 - xh) * NZ + z) * 2 + core, t)
    sib = ((xh * NZ + z) * 2 + 1 - core, t)
    nxt, prv = ((s + 1) % 32, t), ((s + 31) % 32, t)

    def send(src, dst, ssem, rsem, dev):
        pltpu.make_async_remote_copy(
            src_ref=src, dst_ref=dst, send_sem=ssem, recv_sem=rsem, device_id=dev, device_id_type=MESH
        ).start()

    def await_bytes(ref, sem):
        pltpu.make_async_copy(ref, ref, sem).wait()

    load_wi = pltpu.make_async_copy(wi_hbm, wi, lsem.at[0])
    load_wo = pltpu.make_async_copy(wo_hbm, wo, lsem.at[1])
    load_wo.start()
    load_wi.start()

    partners = [tdev(r) for r in RELS] + [zdev(d) for d in range(1, NZ)] + [xdev, nxt, prv]
    barrier = pltpu.get_barrier_semaphore()
    for dev in partners:
        pl.semaphore_signal(barrier, inc=1, device_id=dev, device_id_type=MESH)
    ct[pl.ds(0, 32)] = cot_ref[...]
    halo[1] = field_ref[...]
    pl.semaphore_wait(barrier, len(partners))

    def ag_begin(buf, i):
        own = buf.at[pl.ds(0, 32)]
        send(own, buf.at[pl.ds(POS[7], 32)], ag_s.at[i], ag_r.at[i, 1], zdev(1))
        send(own, buf.at[pl.ds(POS[1], 32)], ag_s.at[i], ag_r.at[i, 2], zdev(-1))
        send(own, buf.at[pl.ds(32, 32)], ag_s.at[i], ag_r.at[i, 0], xdev)
        send(own, buf.at[pl.ds(64, 32)], ag_s.at[i], sib_r.at[i, 0], sib)

    def ag_cross(buf, i):
        got = buf.at[pl.ds(32, 32)]
        await_bytes(got, ag_r.at[i, 0])
        send(got, buf.at[pl.ds(POS[7] + 32, 32)], ag_s.at[i], ag_r.at[i, 3], zdev(1))
        send(got, buf.at[pl.ds(POS[1] + 32, 32)], ag_s.at[i], ag_r.at[i, 4], zdev(-1))
        send(got, buf.at[pl.ds(96, 32)], ag_s.at[i], sib_r.at[i, 0], sib)

    def ag_step(buf, i, j):
        for xr in range(2):
            for way, (dz, ahead, nz) in enumerate(((NZ - j, 1, NZ - j - 1), (j, -1, j + 1))):
                if j == 4 and way != xr:
                    continue
                piece = buf.at[pl.ds(POS[dz] + 32 * xr, 32)]
                await_bytes(piece, ag_r.at[i, 4 * (j - 1) + 1 + 2 * xr + way])
                if j < 3 or (j == 3 and way == xr):
                    send(
                        piece, buf.at[pl.ds(POS[nz] + 32 * xr, 32)], ag_s.at[i],
                        ag_r.at[i, 4 * j + 1 + 2 * xr + way], zdev(ahead),
                    )
        for dz in CHUNK_DZ[j]:
            send(buf.at[pl.ds(POS[dz], 64)], buf.at[pl.ds(POS[dz] + 64, 64)], ag_s.at[i], sib_r.at[i, dz], sib)

    def ag_ready(buf, i, j):
        for dz in CHUNK_DZ[j]:
            await_bytes(buf.at[pl.ds(POS[dz] + 64, 64)], sib_r.at[i, dz])

    def mm(src, w, out, chunk, width, transposed):
        first, length = CHUNKS[chunk]
        left = src.at[pl.ds(first, length)]

        def tile(i, carry):
            at = pl.multiple_of(jnp.minimum(i * 256, width - 256), 128)
            if transposed:
                block = lax.dot_general(
                    left[...], w[pl.ds(at, 256), :], (((1,), (1,)), ((), ())), preferred_element_type=F32
                )
            else:
                block = jnp.dot(left[...], w[:, pl.ds(at, 256)], preferred_element_type=F32)
            out[pl.ds(first, length), pl.ds(at, 256)] = block.astype(BF16)
            return carry

        lax.fori_loop(0, 4, tile, 0)

    def rs_send(part, recv, i, chunk):
        first, length = CHUNKS[chunk]
        w = length // NT
        for slot, rel in enumerate(RELS):
            dev = tdev(rel)
            src = part.at[pl.ds(pl.multiple_of(first + dev[1] * w, w), w)]
            send(src, recv.at[pl.ds(7 * OWN[chunk] + slot * w, w)], rs_s.at[i, chunk], rs_r.at[i, chunk], dev)

    def rs_sum(part, recv, i, chunk):
        first, length = CHUNKS[chunk]
        w = length // NT
        await_bytes(recv.at[pl.ds(7 * OWN[chunk], 7 * w)], rs_r.at[i, chunk])
        total = part[pl.ds(pl.multiple_of(first + t * w, w), w)].astype(F32)
        for slot in range(7):
            total = total + recv[pl.ds(7 * OWN[chunk] + slot * w, w)].astype(F32)
        return total

    def at_send(buf, i, chunk):
        first, length = CHUNKS[chunk]
        w = length // NT
        mine = buf.at[pl.ds(pl.multiple_of(first + t * w, w), w)]
        for rel in RELS:
            send(mine, mine, at_s.at[i, chunk], at_r.at[i, chunk], tdev(rel))

    def at_wait(buf, i, chunk):
        first, length = CHUNKS[chunk]
        await_bytes(buf.at[pl.ds(first, 7 * length // NT)], at_r.at[i, chunk])

    def sc_sibling(part, sb, i, chunk):
        for dz in CHUNK_DZ[chunk]:
            send(part.at[pl.ds(POS[dz] + 64, 64)], sb.at[pl.ds(64 * dz, 64)], sc_s.at[i], sc_sib.at[i, dz], sib)

    def sc_chunk(part, sb, q, rr, i, chunk):
        for dz in CHUNK_DZ[chunk]:
            await_bytes(sb.at[pl.ds(64 * dz, 64)], sc_sib.at[i, dz])
            total = part[pl.ds(POS[dz], 64)].astype(F32) + sb[pl.ds(64 * dz, 64)].astype(F32)
            here = q.at[pl.ds(64 * dz, 64)]
            if dz == 4:
                here[...] = total.astype(BF16)
                send(q.at[pl.ds(256, 32)], rr.at[pl.ds(64 * 3, 32)], sc_s.at[i], sc_ring.at[i, 3], zdev(1))
                send(q.at[pl.ds(288, 32)], rr.at[pl.ds(64 * 5 + 32, 32)], sc_s.at[i], sc_ring.at[i, 5], zdev(-1))
            elif dz in (3, 5):
                here[...] = total.astype(BF16)
                half = 0 if dz == 3 else 32
                more = rr.at[pl.ds(64 * dz + half, 32)]
                await_bytes(more, sc_ring.at[i, dz])
                rows = pl.ds(64 * dz + half, 32)
                q[rows] = (total[half : half + 32] + more[...].astype(F32)).astype(BF16)
            elif dz != 0:
                more = rr.at[pl.ds(64 * dz, 64)]
                await_bytes(more, sc_ring.at[i, dz])
                here[...] = (total + more[...].astype(F32)).astype(BF16)
            if dz in (1, 2, 3):
                to = 8 if dz == 1 else dz - 1
                send(here, rr.at[pl.ds(64 * to, 64)], sc_s.at[i], sc_ring.at[i, to], zdev(1))
            if dz in (5, 6, 7):
                to = 0 if dz == 7 else dz + 1
                send(here, rr.at[pl.ds(64 * to, 64)], sc_s.at[i], sc_ring.at[i, to], zdev(-1))
            if dz == 0:
                for slot in (8, 0):
                    more = rr.at[pl.ds(64 * slot, 64)]
                    await_bytes(more, sc_ring.at[i, slot])
                    total = total + more[...].astype(F32)
                q[pl.ds(32, 32)] = total[32:].astype(BF16)
                return total[:32]

    def sc_cross(q, xr, i):
        send(q.at[pl.ds(32, 32)], xr, sc_s.at[i], sc_x.at[i], xdev)

    send(field_ref, halo.at[0], halo_s.at[0], halo_r.at[0], nxt)
    send(field_ref, halo.at[2], halo_s.at[1], halo_r.at[1], prv)
    ag_begin(ct, 0)
    await_bytes(halo.at[0], halo_r.at[0])
    await_bytes(halo.at[2], halo_r.at[1])

    def conv_tile(i, carry):
        lanes = pl.ds(pl.multiple_of(i * 128, 128), 128)
        rows = [halo[r, :, lanes].astype(F32) for r in range(3)]
        total = jnp.zeros((COLS, 128), F32)
        for k, (dr, dc) in enumerate(OFFSETS):
            moved = rows[1 + dr] if dc == 0 else pltpu.roll(rows[1 + dr], (-dc) % COLS, 0)
            total = total + taps_ref[k : k + 1, lanes] * moved
        mx[pl.ds(0, 32), lanes] = (rows[1] + total).astype(BF16)
        return carry

    lax.fori_loop(0, 8, conv_tile, 0)
    ag_cross(ct, 0)
    ag_begin(mx, 1)
    load_wo.wait()

    for c in range(5):
        if c > 0:
            ag_step(ct, 0, c)
        if c == 1:
            ag_cross(mx, 1)
        if c > 1:
            ag_step(mx, 1, c - 1)
        ag_ready(ct, 0, c)
        mm(ct, wo, gp, c, FB, True)
        rs_send(gp, rg, 0, c)
    store_ct = pltpu.make_async_copy(ct, ct_hbm, lsem.at[2])
    store_ct.start()
    ag_step(mx, 1, 4)
    load_wi.wait()
    for c in range(5):
        ag_ready(mx, 1, c)
    store_mx = pltpu.make_async_copy(mx, mx_hbm, lsem.at[3])
    store_mx.start()
    for c in range(4, -1, -1):
        mm(mx, wi, hp, c, FB, False)
        rs_send(hp, rh, 1, c)
    for c in range(5):
        own_g[pl.ds(OWN[c], CHUNKS[c][1] // NT)] = rs_sum(gp, rg, 0, c)
    for c in range(4, -1, -1):
        first, length = CHUNKS[c]
        w = length // NT
        act, slope = gelu_pair(rs_sum(hp, rh, 1, c))
        rows = pl.ds(pl.multiple_of(first + t * w, w), w)
        hv[rows] = (own_g[pl.ds(OWN[c], w)] * slope).astype(BF16)
        av[rows] = act.astype(BF16)
        at_send(hv, 0, c)
    for c in range(4, -1, -1):
        at_send(av, 1, c)

    mgrow = None
    for c in range(4, -1, -1):
        at_wait(hv, 0, c)
        mm(hv, wi, pm, c, DB, True)
        sc_sibling(pm, sbm, 0, c)
        mgrow = sc_chunk(pm, sbm, qm, rrm, 0, c)
    sc_cross(qm, xrm, 0)
    mg[...] = mgrow
    store_hg = pltpu.make_async_copy(hv, hg_hbm, lsem.at[4])
    store_hg.start()

    def k_stage(i):
        if i == 0:
            await_bytes(xrm, sc_x.at[0])
            mg[...] = mg[...] + xrm[...].astype(F32)
            send(mg, mhalo.at[0], mh_s.at[0], mh_r.at[0], nxt)
            send(mg, mhalo.at[1], mh_s.at[1], mh_r.at[1], prv)

            def kgrad_tile(n, carry):
                lanes = pl.ds(pl.multiple_of(n * 128, 128), 128)
                grad = mg[:, lanes]
                rows = [halo[r, :, lanes].astype(F32) for r in range(3)]
                sums = []
                for dr, dc in OFFSETS:
                    moved = rows[1 + dr] if dc == 0 else pltpu.roll(rows[1 + dr], (-dc) % COLS, 0)
                    sums.append(jnp.sum(grad * moved, axis=0, keepdims=True))
                kp[n] = jnp.concatenate(sums + [jnp.zeros((7, 128), F32)], axis=0)
                return carry

            lax.fori_loop(0, 8, kgrad_tile, 0)
            send(kp, kr.at[0], k_s.at[0], k_r.at[0], sib)
        if i == 1:
            await_bytes(kr.at[0], k_r.at[0])
            await_bytes(kp, k_s.at[0])
            kp[...] = kp[...] + kr[0]
            send(kp, kr.at[1], k_s.at[1], k_r.at[1], xdev)
            await_bytes(mhalo.at[0], mh_r.at[0])
            await_bytes(mhalo.at[1], mh_r.at[1])

            def fgrad_tile(n, carry):
                lanes = pl.ds(pl.multiple_of(n * 128, 128), 128)
                rows = [mhalo[0, :, lanes], mg[:, lanes], mhalo[1, :, lanes]]
                total = rows[1]
                for k, (dr, dc) in enumerate(OFFSETS):
                    moved = rows[1 - dr] if dc == 0 else pltpu.roll(rows[1 - dr], dc % COLS, 0)
                    total = total + taps_ref[k : k + 1, lanes] * moved
                fgrad_ref[:, lanes] = total
                return carry

            lax.fori_loop(0, 8, fgrad_tile, 0)
        if i == 2:
            await_bytes(kr.at[1], k_r.at[1])
            await_bytes(kp, k_s.at[1])
            kp[...] = kp[...] + kr[1]
            for d in range(1, NZ):
                dev = zdev(d)
                send(kp.at[(z + d) % NZ], kz.at[d - 1], k_s.at[2], k_r.at[2], dev)
        if i == 3:
            await_bytes(kz, k_r.at[2])
            total = kp[z]
            for d in range(7):
                total = total + kz[d]
            kf[...] = total
            kg[z] = total
            for d in range(1, NZ):
                send(kf, kg.at[z], k_s.at[3], k_r.at[3], zdev(d))
        if i == 4:
            await_bytes(kg.at[pl.ds(0, 7)], k_r.at[3])
            for n in range(8):
                kgrad_ref[:, 128 * n : 128 * (n + 1)] = kg[n, 0:9] * FACTOR

    row = None
    for c in range(4, -1, -1):
        at_wait(av, 1, c)
        mm(av, wo, pr, c, DB, False)
        sc_sibling(pr, sbr, 1, c)
        if c < 4:
            k_stage(3 - c)
        row = sc_chunk(pr, sbr, qr, rrr, 1, c)
    sc_cross(qr, xrr, 1)
    store_a = pltpu.make_async_copy(av, a_hbm, lsem.at[5])
    store_a.start()
    result_ref[...] = row
    k_stage(4)
    await_bytes(xrr, sc_x.at[1])
    result_ref[...] = result_ref[...] + xrr[...].astype(F32)

    for cp in (store_ct, store_mx, store_hg, store_a):
        cp.wait()
    for i in range(2):
        await_bytes(halo.at[0], halo_s.at[i])
        await_bytes(mhalo.at[0], mh_s.at[i])
        await_bytes(ct.at[pl.ds(0, 992)], ag_s.at[i])
        for c in range(5):
            n = 7 * CHUNKS[c][1] // NT
            await_bytes(gp.at[pl.ds(0, n)], rs_s.at[i, c])
            await_bytes(hv.at[pl.ds(0, n)], at_s.at[i, c])
        await_bytes(pm.at[pl.ds(0, 992)], sc_s.at[i])
    await_bytes(kz, k_s.at[2])
    await_bytes(kz, k_s.at[3])


def on_device(field, w_in, w_out, taps, cotangent):
    vm, hbm = pl.BlockSpec(memory_space=pltpu.VMEM), pl.BlockSpec(memory_space=pl.ANY)
    dma = pltpu.SemaphoreType.DMA
    shapes = [
        ((COLS, DB), F32), ((COLS, DB), F32), ((9, DB), F32),
        ((TOKENS, FB), BF16), ((TOKENS, FB), BF16), ((TOKENS, DB), BF16), ((TOKENS, DB), BF16),
    ]
    scratch = [
        pltpu.VMEM((DB, FB), BF16), pltpu.VMEM((FB, DB), BF16),
        pltpu.VMEM((TOKENS, DB), BF16), pltpu.VMEM((TOKENS, DB), BF16),
        pltpu.VMEM((TOKENS, FB), BF16), pltpu.VMEM((TOKENS, FB), BF16),
        pltpu.VMEM((7 * 128, FB), BF16), pltpu.VMEM((7 * 128, FB), BF16),
        pltpu.VMEM((128, FB), F32),
        pltpu.VMEM((TOKENS, FB), BF16), pltpu.VMEM((TOKENS, FB), BF16),
        pltpu.VMEM((TOKENS, DB), BF16), pltpu.VMEM((TOKENS, DB), BF16),
        pltpu.VMEM((512, DB), BF16), pltpu.VMEM((512, DB), BF16),
        pltpu.VMEM((512, DB), BF16), pltpu.VMEM((512, DB), BF16),
        pltpu.VMEM((576, DB), BF16), pltpu.VMEM((576, DB), BF16),
        pltpu.VMEM((32, DB), BF16), pltpu.VMEM((32, DB), BF16),
        pltpu.VMEM((3, COLS, DB), BF16), pltpu.VMEM((COLS, DB), F32), pltpu.VMEM((2, COLS, DB), F32),
        pltpu.VMEM((8, 16, 128), F32), pltpu.VMEM((2, 8, 16, 128), F32), pltpu.VMEM((7, 16, 128), F32),
        pltpu.VMEM((16, 128), F32), pltpu.VMEM((8, 16, 128), F32),
        dma((6,)), dma((2,)), dma((2,)), dma((2,)), dma((2, 17)), dma((2, 8)),
        dma((2, 5)), dma((2, 5)), dma((2, 5)), dma((2, 5)),
        dma((2,)), dma((2, 8)), dma((2, 9)), dma((2,)), dma((2,)), dma((2,)), dma((4,)), dma((4,)),
    ]
    result, fgrad, kgrad, acts, hgrads, mixed, cots = pl.pallas_call(
        kernel,
        out_shape=[jax.ShapeDtypeStruct(*x) for x in shapes],
        in_specs=[vm, vm, vm, hbm, hbm],
        out_specs=[vm, vm, vm, hbm, hbm, hbm, hbm],
        scratch_shapes=scratch,
        compiler_params=pltpu.CompilerParams(
            collective_id=0, has_side_effects=True, vmem_limit_bytes=60 * 2**20
        ),
        cost_estimate=pl.CostEstimate(flops=4 * 2 * 1024 * 1024 * 896, bytes_accessed=12 * 2**20, transcendentals=0),
        name="block",
    )(field.reshape(COLS, DB), cotangent.reshape(COLS, DB), taps, w_in, w_out)
    grad_out = jnp.einsum("tf,td->fd", acts, cots, preferred_element_type=F32) * FACTOR
    grad_in = jnp.einsum("td,tf->df", mixed, hgrads, preferred_element_type=F32) * FACTOR
    return (result.reshape(1, COLS, DB), fgrad.reshape(1, COLS, DB), grad_in, grad_out, kgrad)


def solution(mesh):
    space = P("space", None, "tensor")
    return jax.shard_map(
        on_device,
        mesh=mesh,
        in_specs=(space, P("tensor", "space"), P("space", "tensor"), P(None, "tensor"), space),
        out_specs=(space, space, P("tensor", "space"), P("space", "tensor"), P(None, "tensor")),
        check_vma=False,
    )
```

```python
import functools
import math

import jax
import jax.numpy as jnp
from jax import lax
from jax.experimental import pallas as pl
from jax.experimental.pallas import tpu as pltpu
from jax.sharding import PartitionSpec as P

MESH = pl.DeviceIdType.MESH
F32, BF16 = jnp.float32, jnp.bfloat16
OFFSETS = [(-1, -1), (-1, 0), (-1, 1), (0, -1), (0, 0), (0, 1), (1, -1), (1, 0), (1, 1)]

NZ, NY, NT = 8, 4, 8
COLS, TOKENS, DB, FB = 32, 1024, 1024, 896
FACTOR = 1.0 / math.sqrt(TOKENS)

ORDER = [0, 1, 7, 2, 6, 3, 5, 4]
POS = {dz: 128 * i for i, dz in enumerate(ORDER)}
CHUNKS = [(0, 128), (128, 256), (384, 256), (640, 256), (896, 128)]
CHUNK_DZ = [[0], [1, 7], [2, 6], [3, 5], [4]]
OWN = [0, 16, 48, 80, 112]
CA = 512
CB = FB - CA
PA, PB = pl.ds(0, CA), pl.ds(CA, CB)


def gelu_pair(hidden):
    c = math.sqrt(2.0 / math.pi)
    square = hidden * hidden
    th = jnp.tanh(c * (hidden + 0.044715 * (square * hidden)))
    half = 0.5 * (1.0 + th)
    slope = half + 0.5 * hidden * (1.0 - th * th) * (c * (1.0 + (3.0 * 0.044715) * square))
    return hidden * half, slope


def kernel(
    field_ref, cot_ref, taps_ref, wi_hbm, wo_hbm,
    result_ref, fgrad_ref, kgrad_ref, gin, gout,
    wi, wo, ct, mx, gp, hp, xa, ya, yain, ybin, xb, xbin, ownb, av, hv,
    pm, pr, sbm, sbr, qm, qr, rrm, rrr, finm, finr, halo, mg, mhalo,
    kp, kr, kz, kf, kg,
    lsem, halo_s, halo_r, ag_s, ag_r, sib_r, rs_s, rs_r, at_s, at_r,
    sc_s, sc_sib, sc_ring, sc_fin, mh_s, mh_r, k_s, k_r,
):
    s, t = lax.axis_index("space"), lax.axis_index("tensor")
    core, z, xh = s % 2, (s // 2) % NZ, s // (2 * NZ)
    y, xl = t // 2, t % 2

    def zdev(dz):
        return ((xh * NZ + (z + dz) % NZ) * 2 + core, t)

    def ydev(dy):
        return (s, ((y + dy) % NY) * 2 + xl)

    def zxdev(dz):
        return (((1 - xh) * NZ + (z + dz) % NZ) * 2 + core, t)

    xdev = (((1 - xh) * NZ + z) * 2 + core, t)
    ldev = (s, y * 2 + 1 - xl)
    sib = ((xh * NZ + z) * 2 + 1 - core, t)
    nxt, prv = ((s + 1) % 32, t), ((s + 31) % 32, t)

    def send(src, dst, ssem, rsem, dev):
        pltpu.make_async_remote_copy(
            src_ref=src, dst_ref=dst, send_sem=ssem, recv_sem=rsem, device_id=dev, device_id_type=MESH
        ).start()

    def await_bytes(ref, sem):
        pltpu.make_async_copy(ref, ref, sem).wait()

    load_wi = pltpu.make_async_copy(wi_hbm, wi, lsem.at[0])
    load_wo = pltpu.make_async_copy(wo_hbm, wo, lsem.at[1])
    load_wo.start()
    load_wi.start()

    partners = [ydev(d) for d in range(1, NY)] + [zdev(d) for d in range(1, NZ)]
    partners += [zxdev(d) for d in range(NZ)] + [ldev, nxt, prv]
    barrier = pltpu.get_barrier_semaphore()
    for dev in partners:
        pl.semaphore_signal(barrier, inc=1, device_id=dev, device_id_type=MESH)
    ct[pl.ds(0, 32)] = cot_ref[...]
    halo[1] = field_ref[...]
    pl.semaphore_wait(barrier, len(partners))

    def ag_begin(buf, i):
        own = buf.at[pl.ds(0, 32)]
        send(own, buf.at[pl.ds(POS[7], 32)], ag_s.at[i], ag_r.at[i, 1], zdev(1))
        send(own, buf.at[pl.ds(POS[1], 32)], ag_s.at[i], ag_r.at[i, 2], zdev(-1))
        send(own, buf.at[pl.ds(32, 32)], ag_s.at[i], ag_r.at[i, 0], xdev)
        send(own, buf.at[pl.ds(64, 32)], ag_s.at[i], sib_r.at[i, 0], sib)

    def ag_cross(buf, i):
        got = buf.at[pl.ds(32, 32)]
        await_bytes(got, ag_r.at[i, 0])
        send(got, buf.at[pl.ds(POS[7] + 32, 32)], ag_s.at[i], ag_r.at[i, 3], zdev(1))
        send(got, buf.at[pl.ds(POS[1] + 32, 32)], ag_s.at[i], ag_r.at[i, 4], zdev(-1))
        send(got, buf.at[pl.ds(96, 32)], ag_s.at[i], sib_r.at[i, 0], sib)

    def ag_step(buf, i, j):
        for xr in range(2):
            for way, (dz, ahead, nz) in enumerate(((NZ - j, 1, NZ - j - 1), (j, -1, j + 1))):
                if j == 4 and way != xr:
                    continue
                piece = buf.at[pl.ds(POS[dz] + 32 * xr, 32)]
                await_bytes(piece, ag_r.at[i, 4 * (j - 1) + 1 + 2 * xr + way])
                if j < 3 or (j == 3 and way == xr):
                    send(
                        piece, buf.at[pl.ds(POS[nz] + 32 * xr, 32)], ag_s.at[i],
                        ag_r.at[i, 4 * j + 1 + 2 * xr + way], zdev(ahead),
                    )
        for dz in CHUNK_DZ[j]:
            send(buf.at[pl.ds(POS[dz], 64)], buf.at[pl.ds(POS[dz] + 64, 64)], ag_s.at[i], sib_r.at[i, dz], sib)

    def ag_ready(buf, i, j):
        for dz in CHUNK_DZ[j]:
            await_bytes(buf.at[pl.ds(POS[dz] + 64, 64)], sib_r.at[i, dz])

    def mm(src, w, out, chunk, transposed):
        first, length = CHUNKS[chunk]
        left = src.at[pl.ds(first, length)]

        if transposed:
            block = lax.dot_general(left[...], w[...], (((1,), (1,)), ((), ())), preferred_element_type=F32)
        else:
            block = jnp.dot(left[...], w[...], preferred_element_type=F32)
        out[pl.ds(first, length)] = block.astype(BF16)

    def rows_of(start, length, w):
        return pl.ds(pl.multiple_of(start, w), length)

    def rs_first(part, i, c):
        first, w = CHUNKS[c][0], CHUNKS[c][1] // NT
        send(
            part.at[rows_of(first + (1 - xl) * 4 * w, 4 * w, w), PA], xa.at[i, pl.ds(4 * OWN[c], 4 * w)],
            rs_s.at[i, c], rs_r.at[i, c, 0], ldev,
        )
        for d in range(1, NY):
            to = (y + d) % NY
            send(
                part.at[rows_of(first + to * 2 * w, 2 * w, w), PB],
                ybin.at[i, pl.ds(6 * OWN[c] + (d - 1) * 2 * w, 2 * w)],
                rs_s.at[i, c], rs_r.at[i, c, 1], ydev(d),
            )

    def rs_second(part, i, c):
        first, w = CHUNKS[c][0], CHUNKS[c][1] // NT
        got = xa.at[i, pl.ds(4 * OWN[c], 4 * w)]
        await_bytes(got, rs_r.at[i, c, 0])
        mine = part[rows_of(first + xl * 4 * w, 4 * w, w), PA].astype(F32)
        ya[i, pl.ds(4 * OWN[c], 4 * w)] = (mine + got[...].astype(F32)).astype(BF16)
        for d in range(1, NY):
            to = (y + d) % NY
            send(
                ya.at[i, rows_of(4 * OWN[c] + to * w, w, w)], yain.at[i, pl.ds(3 * OWN[c] + (d - 1) * w, w)],
                rs_s.at[i, c], rs_r.at[i, c, 2], ydev(d),
            )
        await_bytes(ybin.at[i, pl.ds(6 * OWN[c], 6 * w)], rs_r.at[i, c, 1])
        for own in range(2):
            half = xl if own else 1 - xl
            total = part[rows_of(first + (y * 2 + half) * w, w, w), PB].astype(F32)
            for d in range(3):
                total = total + ybin[i, rows_of(6 * OWN[c] + (2 * d + half) * w, w, w)].astype(F32)
            if own:
                ownb[i, pl.ds(OWN[c], w)] = total
            else:
                xb[i, pl.ds(OWN[c], w)] = total.astype(BF16)
                send(
                    xb.at[i, pl.ds(OWN[c], w)], xbin.at[i, pl.ds(OWN[c], w)],
                    rs_s.at[i, c], rs_r.at[i, c, 3], ldev,
                )

    def rs_final(c):
        first, w = CHUNKS[c][0], CHUNKS[c][1] // NT
        mine = pl.ds(OWN[c], w)
        for i in range(2):
            await_bytes(yain.at[i, pl.ds(3 * OWN[c], 3 * w)], rs_r.at[i, c, 2])
            await_bytes(xbin.at[i, mine], rs_r.at[i, c, 3])

        def store(sums, rows, columns):
            act, slope = gelu_pair(sums[1])
            hv[rows, columns] = (sums[0] * slope).astype(BF16)
            av[rows, columns] = act.astype(BF16)

        sums = []
        for i in range(2):
            total = ya[i, rows_of(4 * OWN[c] + y * w, w, w)].astype(F32)
            for d in range(3):
                total = total + yain[i, pl.ds(3 * OWN[c] + d * w, w)].astype(F32)
            sums.append(total)
        store(sums, rows_of(first + (xl * 4 + y) * w, w, w), PA)
        sums = [ownb[i, mine] + xbin[i, mine].astype(F32) for i in range(2)]
        store(sums, rows_of(first + (y * 2 + xl) * w, w, w), PB)

    def at_first(buf, i, c):
        first, w = CHUNKS[c][0], CHUNKS[c][1] // NT
        piece = buf.at[rows_of(first + (xl * 4 + y) * w, w, w), PA]
        for d in range(1, NY):
            send(piece, piece, at_s.at[i, c], at_r.at[i, c, 0], ydev(d))
        piece = buf.at[rows_of(first + (y * 2 + xl) * w, w, w), PB]
        send(piece, piece, at_s.at[i, c], at_r.at[i, c, 1], ldev)

    def at_second(buf, i, c):
        first, w = CHUNKS[c][0], CHUNKS[c][1] // NT
        await_bytes(buf.at[pl.ds(first, w), PB], at_r.at[i, c, 1])
        piece = buf.at[rows_of(first + y * 2 * w, 2 * w, w), PB]
        for d in range(1, NY):
            send(piece, piece, at_s.at[i, c], at_r.at[i, c, 3], ydev(d))
        await_bytes(buf.at[pl.ds(first, 3 * w), PA], at_r.at[i, c, 0])
        piece = buf.at[rows_of(first + xl * 4 * w, 4 * w, w), PA]
        send(piece, piece, at_s.at[i, c], at_r.at[i, c, 2], ldev)

    def at_wait(buf, i, c):
        first, w = CHUNKS[c][0], CHUNKS[c][1] // NT
        await_bytes(buf.at[pl.ds(first, 4 * w), PA], at_r.at[i, c, 2])
        await_bytes(buf.at[pl.ds(first, 6 * w), PB], at_r.at[i, c, 3])

    def grad_tile(left, right, out, n):
        block = lax.dot_general(
            left[:, 128 * n : 128 * (n + 1)], right[...], (((0,), (0,)), ((), ())), preferred_element_type=F32
        )
        out[pl.ds(128 * n, 128)] = block * FACTOR

    def grad_in(lo, hi):
        for n in range(lo, hi):
            grad_tile(mx, hv, gin, n)

    def grad_out(lo, hi):
        for n in range(lo, hi):
            grad_tile(av, ct, gout, n)

    def sc_sibling(part, sb, i, chunk):
        for dz in CHUNK_DZ[chunk]:
            send(part.at[pl.ds(POS[dz] + 64, 64)], sb.at[pl.ds(64 * dz, 64)], sc_s.at[i], sc_sib.at[i, dz], sib)

    def sc_piece(part, sb, q, rr, fin, i, dz, xr):
        rows = pl.ds(64 * dz + 32 * xr, 32)
        total = part[pl.ds(POS[dz] + 32 * xr, 32)].astype(F32) + sb[rows].astype(F32)
        if dz in (1, 2, 6, 7) or (dz, xr) in ((3, 0), (5, 1)):
            await_bytes(rr.at[rows], sc_ring.at[i, 2 * dz + xr])
            total = total + rr[rows].astype(F32)
        q[rows] = total.astype(BF16)
        way = 1 if dz < 4 or (dz == 4 and xr == 0) else -1
        if dz in (1, 7):
            slot = (0 if dz == 1 else 2) + xr
            dev = zxdev(way) if xr else zdev(way)
            send(q.at[rows], fin.at[slot], sc_s.at[i], sc_fin.at[i, slot], dev)
        else:
            to = 64 * (dz - way) + 32 * xr
            send(q.at[rows], rr.at[pl.ds(to, 32)], sc_s.at[i], sc_ring.at[i, 2 * (dz - way) + xr], zdev(way))

    def sc_chunk(part, sb, q, rr, fin, i, chunk):
        for dz in CHUNK_DZ[chunk]:
            await_bytes(sb.at[pl.ds(64 * dz, 64)], sc_sib.at[i, dz])
        if chunk == 4:
            order = [(4, 0), (4, 1)]
        else:
            order = [(chunk, 1), (NZ - chunk, 0), (chunk, 0), (NZ - chunk, 1)]
        for dz, xr in order:
            sc_piece(part, sb, q, rr, fin, i, dz, xr)

    def sc_own(part, sb, q, fin, i):
        await_bytes(sb.at[pl.ds(0, 64)], sc_sib.at[i, 0])
        q[pl.ds(32, 32)] = (part[pl.ds(32, 32)].astype(F32) + sb[pl.ds(32, 32)].astype(F32)).astype(BF16)
        send(q.at[pl.ds(32, 32)], fin.at[4], sc_s.at[i], sc_fin.at[i, 4], xdev)

    def sc_total(part, sb, fin, i):
        total = part[pl.ds(0, 32)].astype(F32) + sb[pl.ds(0, 32)].astype(F32)
        for slot in (4, 1, 3, 0, 2):
            await_bytes(fin.at[slot], sc_fin.at[i, slot])
            total = total + fin[slot].astype(F32)
        return total

    send(field_ref, halo.at[0], halo_s.at[0], halo_r.at[0], nxt)
    send(field_ref, halo.at[2], halo_s.at[1], halo_r.at[1], prv)
    ag_begin(ct, 0)
    await_bytes(halo.at[0], halo_r.at[0])
    await_bytes(halo.at[2], halo_r.at[1])

    def conv_tile(i, carry):
        lanes = pl.ds(pl.multiple_of(i * 128, 128), 128)
        rows = [halo[r, :, lanes].astype(F32) for r in range(3)]
        total = jnp.zeros((COLS, 128), F32)
        for k, (dr, dc) in enumerate(OFFSETS):
            moved = rows[1 + dr] if dc == 0 else pltpu.roll(rows[1 + dr], (-dc) % COLS, 0)
            total = total + taps_ref[k : k + 1, lanes] * moved
        mx[pl.ds(0, 32), lanes] = (rows[1] + total).astype(BF16)
        return carry

    lax.fori_loop(0, 8, conv_tile, 0)
    ag_cross(ct, 0)
    ag_begin(mx, 1)
    load_wo.wait()
    for c in range(5):
        if c > 0:
            ag_step(ct, 0, c)
        ag_ready(ct, 0, c)
        mm(ct, wo, gp, c, True)
        rs_first(gp, 0, c)
        if c > 0:
            ag_step(mx, 1, c)
        else:
            ag_cross(mx, 1)
            load_wi.wait()
        ag_ready(mx, 1, c)
        mm(mx, wi, hp, c, False)
        rs_first(hp, 1, c)
        if c > 0:
            rs_second(gp, 0, c - 1)
            rs_second(hp, 1, c - 1)
        if c > 1:
            rs_final(c - 2)
    rs_second(gp, 0, 4)
    rs_second(hp, 1, 4)

    def mgrad_part(c):
        at_wait(hv, 0, c)
        mm(hv, wi, pm, c, True)
        sc_sibling(pm, sbm, 0, c)

    def result_part(c):
        at_wait(av, 1, c)
        mm(av, wo, pr, c, False)
        sc_sibling(pr, sbr, 1, c)

    def mgrad_sum(c):
        sc_chunk(pm, sbm, qm, rrm, finm, 0, c)

    def result_sum(c):
        sc_chunk(pr, sbr, qr, rrr, finr, 1, c)

    def k_stage(i):
        if i == 0:
            send(mg, mhalo.at[0], mh_s.at[0], mh_r.at[0], nxt)
            send(mg, mhalo.at[1], mh_s.at[1], mh_r.at[1], prv)

            def kgrad_tile(n, carry):
                lanes = pl.ds(pl.multiple_of(n * 128, 128), 128)
                grad = mg[:, lanes]
                rows = [halo[r, :, lanes].astype(F32) for r in range(3)]
                sums = []
                for dr, dc in OFFSETS:
                    moved = rows[1 + dr] if dc == 0 else pltpu.roll(rows[1 + dr], (-dc) % COLS, 0)
                    sums.append(jnp.sum(grad * moved, axis=0, keepdims=True))
                kp[n] = jnp.concatenate(sums + [jnp.zeros((7, 128), F32)], axis=0)
                return carry

            lax.fori_loop(0, 8, kgrad_tile, 0)
            send(kp, kr, k_s.at[0], k_r.at[0], sib)
        if i == 1:
            await_bytes(kr, k_r.at[0])
            await_bytes(kp, k_s.at[0])
            kp[...] = kp[...] + kr[...]
            for n, d in enumerate(list(range(1, NZ)) + list(range(NZ))):
                dev = zdev(d) if n < 7 else zxdev(d)
                send(kp.at[(z + d) % NZ], kz.at[n], k_s.at[1], k_r.at[1], dev)
            await_bytes(mhalo.at[0], mh_r.at[0])
            await_bytes(mhalo.at[1], mh_r.at[1])

            def fgrad_tile(n, carry):
                lanes = pl.ds(pl.multiple_of(n * 128, 128), 128)
                rows = [mhalo[0, :, lanes], mg[:, lanes], mhalo[1, :, lanes]]
                total = rows[1]
                for k, (dr, dc) in enumerate(OFFSETS):
                    moved = rows[1 - dr] if dc == 0 else pltpu.roll(rows[1 - dr], dc % COLS, 0)
                    total = total + taps_ref[k : k + 1, lanes] * moved
                fgrad_ref[:, lanes] = total
                return carry

            lax.fori_loop(0, 8, fgrad_tile, 0)
        if i == 2:
            await_bytes(kz, k_r.at[1])
            total = kp[z]
            for n in range(15):
                total = total + kz[n]
            kf[...] = total
            kg[z] = total
            for d in range(1, NZ):
                send(kf, kg.at[z], k_s.at[2], k_r.at[2], zdev(d))
        if i == 3:
            await_bytes(kg.at[pl.ds(0, 7)], k_r.at[2])
            for n in range(8):
                kgrad_ref[:, 128 * n : 128 * (n + 1)] = kg[n, 0:9] * FACTOR

    at_first(hv, 0, 0)
    at_first(hv, 0, 1)
    at_first(hv, 0, 2)
    rs_final(3)
    rs_final(4)
    at_first(hv, 0, 4)
    at_first(hv, 0, 3)
    at_second(hv, 0, 0)
    at_second(hv, 0, 4)
    at_second(hv, 0, 3)
    at_first(av, 1, 4)
    at_second(hv, 0, 1)
    at_second(hv, 0, 2)
    at_first(av, 1, 3)
    mgrad_part(0)
    mgrad_part(4)
    sc_own(pm, sbm, qm, finm, 0)
    mgrad_sum(4)
    mgrad_part(1)
    mgrad_part(3)
    at_second(av, 1, 4)
    at_first(av, 1, 2)
    mgrad_sum(3)
    mgrad_part(2)
    at_second(av, 1, 3)
    at_first(av, 1, 1)
    result_part(4)
    mgrad_sum(2)
    result_sum(4)
    result_part(3)
    at_second(av, 1, 2)
    at_first(av, 1, 0)
    grad_in(0, 2)
    mgrad_sum(1)
    result_sum(3)
    result_part(2)
    at_second(av, 1, 1)
    mg[...] = sc_total(pm, sbm, finm, 0)
    k_stage(0)
    result_sum(2)
    result_part(1)
    k_stage(1)
    at_second(av, 1, 0)
    grad_in(2, 8)
    result_sum(1)
    k_stage(2)
    result_part(0)
    sc_own(pr, sbr, qr, finr, 1)
    grad_out(0, 7)
    result_ref[...] = sc_total(pr, sbr, finr, 1)
    k_stage(3)

    for i in range(2):
        await_bytes(halo.at[0], halo_s.at[i])
        await_bytes(mhalo.at[0], mh_s.at[i])
        await_bytes(ct.at[pl.ds(0, 992)], ag_s.at[i])
        for c in range(5):
            n = 7 * CHUNKS[c][1] // NT
            await_bytes(gp.at[pl.ds(0, n)], rs_s.at[i, c])
            await_bytes(hv.at[pl.ds(0, n)], at_s.at[i, c])
        await_bytes(pm.at[pl.ds(0, 992)], sc_s.at[i])
    await_bytes(kz, k_s.at[1])
    await_bytes(kg.at[pl.ds(0, 7)], k_s.at[2])


def write_out(*refs):
    copies = [pltpu.make_async_copy(refs[i], refs[5 + i], refs[10].at[i]) for i in range(5)]
    for cp in copies:
        cp.start()
    for cp in copies:
        cp.wait()


def on_device(field, w_in, w_out, taps, cotangent):
    vm, hbm = pl.BlockSpec(memory_space=pltpu.VMEM), pl.BlockSpec(memory_space=pl.ANY)
    dma = pltpu.SemaphoreType.DMA
    shapes = [
        ((COLS, DB), F32), ((COLS, DB), F32), ((9, DB), F32),
        ((DB, FB), F32), ((FB, DB), F32),
    ]
    scratch = [
        pltpu.VMEM((DB, FB), BF16), pltpu.VMEM((FB, DB), BF16),
        pltpu.VMEM((TOKENS, DB), BF16), pltpu.VMEM((TOKENS, DB), BF16),
        pltpu.VMEM((TOKENS, FB), BF16), pltpu.VMEM((TOKENS, FB), BF16),
        pltpu.VMEM((2, 512, CA), BF16), pltpu.VMEM((2, 512, CA), BF16), pltpu.VMEM((2, 384, CA), BF16),
        pltpu.VMEM((2, 768, CB), BF16), pltpu.VMEM((2, 128, CB), BF16), pltpu.VMEM((2, 128, CB), BF16),
        pltpu.VMEM((2, 128, CB), F32),
        pltpu.VMEM((TOKENS, FB), BF16), pltpu.VMEM((TOKENS, FB), BF16),
        pltpu.VMEM((TOKENS, DB), BF16), pltpu.VMEM((TOKENS, DB), BF16),
        pltpu.VMEM((512, DB), BF16), pltpu.VMEM((512, DB), BF16),
        pltpu.VMEM((512, DB), BF16), pltpu.VMEM((512, DB), BF16),
        pltpu.VMEM((512, DB), BF16), pltpu.VMEM((512, DB), BF16),
        pltpu.VMEM((5, 32, DB), BF16), pltpu.VMEM((5, 32, DB), BF16),
        pltpu.VMEM((3, COLS, DB), BF16), pltpu.VMEM((COLS, DB), F32), pltpu.VMEM((2, COLS, DB), F32),
        pltpu.VMEM((8, 16, 128), F32), pltpu.VMEM((8, 16, 128), F32), pltpu.VMEM((15, 16, 128), F32),
        pltpu.VMEM((16, 128), F32), pltpu.VMEM((8, 16, 128), F32),
        dma((2,)), dma((2,)), dma((2,)), dma((2,)), dma((2, 17)), dma((2, 8)),
        dma((2, 5)), dma((2, 5, 4)), dma((2, 5)), dma((2, 5, 4)),
        dma((2,)), dma((2, 8)), dma((2, 16)), dma((2, 5)), dma((2,)), dma((2,)), dma((3,)), dma((3,)),
    ]
    held = pl.pallas_call(
        kernel,
        out_shape=[pltpu.VMEM(*x) for x in shapes],
        in_specs=[vm, vm, vm, hbm, hbm],
        out_specs=[vm] * 5,
        scratch_shapes=scratch,
        compiler_params=pltpu.CompilerParams(
            collective_id=0, has_side_effects=True, vmem_limit_bytes=48 * 2**20
        ),
        cost_estimate=pl.CostEstimate(flops=6 * 2 * 1024 * 1024 * 896, bytes_accessed=12 * 2**20, transcendentals=0),
        name="block",
    )(field.reshape(COLS, DB), cotangent.reshape(COLS, DB), taps, w_in, w_out)
    result, fgrad, kgrad, grad_in, grad_out = pl.pallas_call(
        write_out,
        out_shape=[jax.ShapeDtypeStruct(*x) for x in shapes],
        in_specs=[hbm] * 5,
        out_specs=[pl.BlockSpec(memory_space=pltpu.HBM)] * 5,
        scratch_shapes=[dma((5,))],
        compiler_params=pltpu.CompilerParams(vmem_limit_bytes=2**20),
        name="write_out",
    )(*held)
    return (result.reshape(1, COLS, DB), fgrad.reshape(1, COLS, DB), grad_in, grad_out, kgrad)


def solution(mesh):
    space = P("space", None, "tensor")
    return jax.shard_map(
        on_device,
        mesh=mesh,
        in_specs=(space, P("tensor", "space"), P("space", "tensor"), P(None, "tensor"), space),
        out_specs=(space, space, P("tensor", "space"), P("space", "tensor"), P(None, "tensor")),
        check_vma=False,
    )
```

```python
import functools
import math

import jax
import jax.numpy as jnp
from jax import lax
from jax.experimental import pallas as pl
from jax.experimental.pallas import tpu as pltpu
from jax.sharding import PartitionSpec as P

MESH = pl.DeviceIdType.MESH
F32, BF16 = jnp.float32, jnp.bfloat16
OFFSETS = [(-1, -1), (-1, 0), (-1, 1), (0, -1), (0, 0), (0, 1), (1, -1), (1, 0), (1, 1)]

NZ, NY, NT = 8, 4, 8
COLS, TOKENS, DB, FB = 32, 1024, 1024, 896
FACTOR = 1.0 / math.sqrt(TOKENS)

ORDER = [0, 1, 7, 2, 6, 3, 5, 4]
POS = {dz: 128 * i for i, dz in enumerate(ORDER)}
CHUNKS = [(0, 128), (128, 256), (384, 256), (640, 256), (896, 128)]
CHUNK_DZ = [[0], [1, 7], [2, 6], [3, 5], [4]]
OWN = [0, 16, 48, 80, 112]
RING = [(3, 0), (5, 1)] + [(dz, xr) for dz in (1, 2, 6, 7) for xr in range(2)]
CA = 512
CB = FB - CA
PA, PB = pl.ds(0, CA), pl.ds(CA, CB)


def gelu_pair(hidden):
    c = math.sqrt(2.0 / math.pi)
    square = hidden * hidden
    th = jnp.tanh(c * (hidden + 0.044715 * (square * hidden)))
    half = 0.5 * (1.0 + th)
    slope = half + 0.5 * hidden * (1.0 - th * th) * (c * (1.0 + (3.0 * 0.044715) * square))
    return hidden * half, slope


def kernel(
    field_hbm, cot_hbm, taps_hbm, wi_hbm, wo_hbm,
    result_ref, fgrad_ref, kgrad_ref, gin, gout,
    taps_ref, wi, wo, ct, mx, gp, hp, xa, ya, yain, ybin, xb, xbin, ownb, av, hv,
    pm, pr, sbm, sbr, qm, qr, rrm, rrr, finm, finr, halo, mg, mhalo,
    kp, kr, kz, kf, kg,
    lsem, halo_s, halo_r, ag_s, ag_r, sib_r, rs_s, rs_r, at_s, at_r,
    sc_s, sc_sib, sc_ring, sc_fin, mh_s, mh_r, k_s, k_r,
):
    s, t = lax.axis_index("space"), lax.axis_index("tensor")
    core, z, xh = s % 2, (s // 2) % NZ, s // (2 * NZ)
    y, xl = t // 2, t % 2

    def zdev(dz):
        return ((xh * NZ + (z + dz) % NZ) * 2 + core, t)

    def ydev(dy):
        return (s, ((y + dy) % NY) * 2 + xl)

    def zxdev(dz):
        return (((1 - xh) * NZ + (z + dz) % NZ) * 2 + core, t)

    xdev = (((1 - xh) * NZ + z) * 2 + core, t)
    ldev = (s, y * 2 + 1 - xl)
    sib = ((xh * NZ + z) * 2 + 1 - core, t)
    nxt, prv = ((s + 1) % 32, t), ((s + 31) % 32, t)

    def send(src, dst, ssem, rsem, dev):
        pltpu.make_async_remote_copy(
            src_ref=src, dst_ref=dst, send_sem=ssem, recv_sem=rsem, device_id=dev, device_id_type=MESH
        ).start()

    def await_bytes(ref, sem):
        pltpu.make_async_copy(ref, ref, sem).wait()

    load_wi = pltpu.make_async_copy(wi_hbm, wi, lsem.at[0])
    load_wo = pltpu.make_async_copy(wo_hbm, wo, lsem.at[1])
    loads = [
        pltpu.make_async_copy(cot_hbm, ct.at[pl.ds(0, 32)], lsem.at[2]),
        pltpu.make_async_copy(field_hbm, halo.at[1], lsem.at[3]),
        pltpu.make_async_copy(taps_hbm, taps_ref, lsem.at[4]),
    ]
    for cp in loads:
        cp.start()
    load_wo.start()
    load_wi.start()

    partners = [ydev(d) for d in range(1, NY)] + [zdev(d) for d in range(1, NZ)]
    partners += [zxdev(d) for d in range(NZ)] + [ldev, nxt, prv]
    barrier = pltpu.get_barrier_semaphore()
    for dev in partners:
        pl.semaphore_signal(barrier, inc=1, device_id=dev, device_id_type=MESH)
    for cp in loads:
        cp.wait()
    pl.semaphore_wait(barrier, len(partners))

    def ag_begin(buf, i):
        own = buf.at[pl.ds(0, 32)]
        send(own, buf.at[pl.ds(POS[7], 32)], ag_s.at[i], ag_r.at[i, 1], zdev(1))
        send(own, buf.at[pl.ds(POS[1], 32)], ag_s.at[i], ag_r.at[i, 2], zdev(-1))
        send(own, buf.at[pl.ds(32, 32)], ag_s.at[i], ag_r.at[i, 0], xdev)
        send(own, buf.at[pl.ds(64, 32)], ag_s.at[i], sib_r.at[i, 0], sib)

    def ag_cross(buf, i):
        got = buf.at[pl.ds(32, 32)]
        await_bytes(got, ag_r.at[i, 0])
        send(got, buf.at[pl.ds(POS[7] + 32, 32)], ag_s.at[i], ag_r.at[i, 3], zdev(1))
        send(got, buf.at[pl.ds(POS[1] + 32, 32)], ag_s.at[i], ag_r.at[i, 4], zdev(-1))
        send(got, buf.at[pl.ds(96, 32)], ag_s.at[i], sib_r.at[i, 0], sib)

    def ag_step(buf, i, j):
        for xr in range(2):
            for way, (dz, ahead, nz) in enumerate(((NZ - j, 1, NZ - j - 1), (j, -1, j + 1))):
                if j == 4 and way != xr:
                    continue
                piece = buf.at[pl.ds(POS[dz] + 32 * xr, 32)]
                await_bytes(piece, ag_r.at[i, 4 * (j - 1) + 1 + 2 * xr + way])
                if j < 3 or (j == 3 and way == xr):
                    send(
                        piece, buf.at[pl.ds(POS[nz] + 32 * xr, 32)], ag_s.at[i],
                        ag_r.at[i, 4 * j + 1 + 2 * xr + way], zdev(ahead),
                    )
        for dz in CHUNK_DZ[j]:
            send(buf.at[pl.ds(POS[dz], 64)], buf.at[pl.ds(POS[dz] + 64, 64)], ag_s.at[i], sib_r.at[i, j], sib)

    def ag_ready(buf, i, j):
        await_bytes(buf.at[pl.ds(0, CHUNKS[j][1] // 2)], sib_r.at[i, j])

    def mm(src, w, out, chunk, transposed):
        first, length = CHUNKS[chunk]
        left = src.at[pl.ds(first, length)]

        if transposed:
            block = lax.dot_general(left[...], w[...], (((1,), (1,)), ((), ())), preferred_element_type=F32)
        else:
            block = jnp.dot(left[...], w[...], preferred_element_type=F32)
        out[pl.ds(first, length)] = block.astype(BF16)

    def rows_of(start, length, w):
        return pl.ds(pl.multiple_of(start, w), length)

    def rs_first(part, i, c):
        first, w = CHUNKS[c][0], CHUNKS[c][1] // NT
        send(
            part.at[rows_of(first + (1 - xl) * 4 * w, 4 * w, w), PA], xa.at[i, pl.ds(4 * OWN[c], 4 * w)],
            rs_s.at[i], rs_r.at[i, c], ldev,
        )
        for d in range(1, NY):
            to = (y + d) % NY
            send(
                part.at[rows_of(first + to * 2 * w, 2 * w, w), PB],
                ybin.at[i, pl.ds(6 * OWN[c] + (d - 1) * 2 * w, 2 * w)],
                rs_s.at[i], rs_r.at[i, c], ydev(d),
            )

    def rs_second(part, i, c):
        first, w = CHUNKS[c][0], CHUNKS[c][1] // NT
        got = xa.at[i, pl.ds(4 * OWN[c], 4 * w)]
        await_bytes(gp.at[pl.ds(0, 17 * w), pl.ds(0, 256)], rs_r.at[i, c])
        mine = part[rows_of(first + xl * 4 * w, 4 * w, w), PA].astype(F32)
        ya[i, pl.ds(4 * OWN[c], 4 * w)] = (mine + got[...].astype(F32)).astype(BF16)
        for d in range(1, NY):
            to = (y + d) % NY
            send(
                ya.at[i, rows_of(4 * OWN[c] + to * w, w, w)], yain.at[i, pl.ds(3 * OWN[c] + (d - 1) * w, w)],
                rs_s.at[i], rs_r.at[2, c], ydev(d),
            )
        for own in range(2):
            half = xl if own else 1 - xl
            total = part[rows_of(first + (y * 2 + half) * w, w, w), PB].astype(F32)
            for d in range(3):
                total = total + ybin[i, rows_of(6 * OWN[c] + (2 * d + half) * w, w, w)].astype(F32)
            if own:
                ownb[i, pl.ds(OWN[c], w)] = total
            else:
                xb[i, pl.ds(OWN[c], w)] = total.astype(BF16)
                send(
                    xb.at[i, pl.ds(OWN[c], w)], xbin.at[i, pl.ds(OWN[c], w)],
                    rs_s.at[i], rs_r.at[2, c], ldev,
                )

    def rs_final(c):
        first, w = CHUNKS[c][0], CHUNKS[c][1] // NT
        mine = pl.ds(OWN[c], w)
        await_bytes(gp.at[pl.ds(0, 15 * w), pl.ds(0, 256)], rs_r.at[2, c])

        def store(sums, rows, columns):
            act, slope = gelu_pair(sums[1])
            hv[rows, columns] = (sums[0] * slope).astype(BF16)
            av[rows, columns] = act.astype(BF16)

        sums = []
        for i in range(2):
            total = ya[i, rows_of(4 * OWN[c] + y * w, w, w)].astype(F32)
            for d in range(3):
                total = total + yain[i, pl.ds(3 * OWN[c] + d * w, w)].astype(F32)
            sums.append(total)
        store(sums, rows_of(first + (xl * 4 + y) * w, w, w), PA)
        sums = [ownb[i, mine] + xbin[i, mine].astype(F32) for i in range(2)]
        store(sums, rows_of(first + (y * 2 + xl) * w, w, w), PB)

    def at_first(buf, i, c):
        first, w = CHUNKS[c][0], CHUNKS[c][1] // NT
        piece = buf.at[rows_of(first + (xl * 4 + y) * w, w, w), PA]
        for d in range(1, NY):
            send(piece, piece, at_s.at[i], at_r.at[i, c, 0], ydev(d))
        piece = buf.at[rows_of(first + (y * 2 + xl) * w, w, w), PB]
        send(piece, piece, at_s.at[i], at_r.at[i, c, 0], ldev)

    def at_second(buf, i, c):
        first, w = CHUNKS[c][0], CHUNKS[c][1] // NT
        await_bytes(gp.at[pl.ds(0, 5 * w), PB], at_r.at[i, c, 0])
        piece = buf.at[rows_of(first + y * 2 * w, 2 * w, w), PB]
        for d in range(1, NY):
            send(piece, piece, at_s.at[i], at_r.at[i, c, 1], ydev(d))
        piece = buf.at[rows_of(first + xl * 4 * w, 4 * w, w), PA]
        send(piece, piece, at_s.at[i], at_r.at[i, c, 1], ldev)

    def at_wait(buf, i, c):
        first, w = CHUNKS[c][0], CHUNKS[c][1] // NT
        await_bytes(gp.at[pl.ds(0, 17 * w), pl.ds(0, 256)], at_r.at[i, c, 1])

    def grad_tile(left, right, out, n):
        block = lax.dot_general(
            left[:, 128 * n : 128 * (n + 1)], right[...], (((0,), (0,)), ((), ())), preferred_element_type=F32
        )
        out[pl.ds(128 * n, 128)] = block * FACTOR

    def grad_in(lo, hi):
        for n in range(lo, hi):
            grad_tile(mx, hv, gin, n)

    def grad_out(lo, hi):
        for n in range(lo, hi):
            grad_tile(av, ct, gout, n)

    def sc_sibling(part, sb, i, chunk):
        for dz in CHUNK_DZ[chunk]:
            send(part.at[pl.ds(POS[dz] + 64, 64)], sb.at[pl.ds(64 * dz, 64)], sc_s.at[i], sc_sib.at[i, chunk], sib)

    def sc_piece(part, sb, q, rr, fin, i, dz, xr):
        rows = pl.ds(64 * dz + 32 * xr, 32)
        total = part[pl.ds(POS[dz] + 32 * xr, 32)].astype(F32) + sb[rows].astype(F32)
        if (dz, xr) in RING:
            await_bytes(rr.at[rows], sc_ring.at[i, RING.index((dz, xr))])
            total = total + rr[rows].astype(F32)
        q[rows] = total.astype(BF16)
        way = 1 if dz < 4 or (dz == 4 and xr == 0) else -1
        if dz in (1, 7):
            slot = (0 if dz == 1 else 2) + xr
            dev = zxdev(way) if xr else zdev(way)
            send(q.at[rows], fin.at[slot], sc_s.at[i], sc_fin.at[i], dev)
        else:
            to = 64 * (dz - way) + 32 * xr
            send(q.at[rows], rr.at[pl.ds(to, 32)], sc_s.at[i], sc_ring.at[i, RING.index((dz - way, xr))], zdev(way))

    def sc_chunk(part, sb, q, rr, fin, i, chunk, late):
        if not late:
            await_bytes(sb.at[pl.ds(0, CHUNKS[chunk][1] // 2)], sc_sib.at[i, chunk])
        for dz, xr in ((chunk, 1 - late), (NZ - chunk, late)):
            sc_piece(part, sb, q, rr, fin, i, dz, xr)

    def sc_own(part, sb, q, fin, i):
        await_bytes(sb.at[pl.ds(0, 64)], sc_sib.at[i, 0])
        q[pl.ds(32, 32)] = (part[pl.ds(32, 32)].astype(F32) + sb[pl.ds(32, 32)].astype(F32)).astype(BF16)
        send(q.at[pl.ds(32, 32)], fin.at[4], sc_s.at[i], sc_fin.at[i], xdev)

    def sc_total(part, sb, fin, i):
        total = part[pl.ds(0, 32)].astype(F32) + sb[pl.ds(0, 32)].astype(F32)
        await_bytes(fin, sc_fin.at[i])
        for slot in range(5):
            total = total + fin[slot].astype(F32)
        return total

    send(halo.at[1], halo.at[0], halo_s, halo_r, nxt)
    send(halo.at[1], halo.at[2], halo_s, halo_r, prv)
    ag_begin(ct, 0)
    await_bytes(halo.at[pl.ds(0, 2)], halo_r)

    def conv_tile(i, carry):
        lanes = pl.ds(pl.multiple_of(i * 128, 128), 128)
        rows = [halo[r, :, lanes].astype(F32) for r in range(3)]
        total = jnp.zeros((COLS, 128), F32)
        for k, (dr, dc) in enumerate(OFFSETS):
            moved = rows[1 + dr] if dc == 0 else pltpu.roll(rows[1 + dr], (-dc) % COLS, 0)
            total = total + taps_ref[k : k + 1, lanes] * moved
        mx[pl.ds(0, 32), lanes] = (rows[1] + total).astype(BF16)
        return carry

    lax.fori_loop(0, 8, conv_tile, 0)
    ag_cross(ct, 0)
    ag_begin(mx, 1)
    load_wo.wait()
    def cot_chunk(c):
        if c > 0:
            ag_step(ct, 0, c)
        ag_ready(ct, 0, c)
        mm(ct, wo, gp, c, True)
        rs_first(gp, 0, c)

    def mixed_chunk(c):
        if c > 0:
            ag_step(mx, 1, c)
        else:
            ag_cross(mx, 1)
            load_wi.wait()
        ag_ready(mx, 1, c)
        mm(mx, wi, hp, c, False)
        rs_first(hp, 1, c)

    cot_chunk(0)
    for c in range(5):
        if c < 4:
            cot_chunk(c + 1)
        mixed_chunk(c)
        if c > 0:
            rs_second(gp, 0, c - 1)
            rs_second(hp, 1, c - 1)
        if c > 1:
            rs_final(c - 2)
    rs_second(gp, 0, 4)
    rs_second(hp, 1, 4)

    def mgrad_part(c):
        at_wait(hv, 0, c)
        mm(hv, wi, pm, c, True)
        sc_sibling(pm, sbm, 0, c)

    def result_part(c):
        at_wait(av, 1, c)
        mm(av, wo, pr, c, False)
        sc_sibling(pr, sbr, 1, c)

    def mgrad_sum(c, late):
        sc_chunk(pm, sbm, qm, rrm, finm, 0, c, late)

    def result_sum(c, late):
        sc_chunk(pr, sbr, qr, rrr, finr, 1, c, late)

    def k_stage(i):
        if i == 0:
            send(mg, mhalo.at[0], mh_s, mh_r, nxt)
            send(mg, mhalo.at[1], mh_s, mh_r, prv)

            def kgrad_tile(n, carry):
                lanes = pl.ds(pl.multiple_of(n * 128, 128), 128)
                grad = mg[:, lanes]
                rows = [halo[r, :, lanes].astype(F32) for r in range(3)]
                sums = []
                for dr, dc in OFFSETS:
                    moved = rows[1 + dr] if dc == 0 else pltpu.roll(rows[1 + dr], (-dc) % COLS, 0)
                    sums.append(jnp.sum(grad * moved, axis=0, keepdims=True))
                kp[n] = jnp.concatenate(sums + [jnp.zeros((7, 128), F32)], axis=0)
                return carry

            lax.fori_loop(0, 8, kgrad_tile, 0)
            send(kp, kr, k_s.at[0], k_r.at[0], sib)
        if i == 1:
            await_bytes(kr, k_r.at[0])
            await_bytes(kp, k_s.at[0])
            kp[...] = kp[...] + kr[...]
            for d in range(1, NZ):
                send(kp.at[(z + d) % NZ], kz.at[d - 1], k_s.at[1], k_r.at[1], zdev(d))
        if i == 4:
            await_bytes(mhalo, mh_r)

            def fgrad_tile(n, carry):
                lanes = pl.ds(pl.multiple_of(n * 128, 128), 128)
                rows = [mhalo[0, :, lanes], mg[:, lanes], mhalo[1, :, lanes]]
                total = rows[1]
                for k, (dr, dc) in enumerate(OFFSETS):
                    moved = rows[1 - dr] if dc == 0 else pltpu.roll(rows[1 - dr], dc % COLS, 0)
                    total = total + taps_ref[k : k + 1, lanes] * moved
                fgrad_ref[:, lanes] = total
                return carry

            lax.fori_loop(0, 8, fgrad_tile, 0)
        if i == 2:
            await_bytes(kz, k_r.at[1])
            total = kp[z]
            for n in range(7):
                total = total + kz[n]
            kf[...] = total
            kg[z] = total
            for d in range(NZ):
                if d > 0:
                    send(kf, kg.at[z], k_s.at[2], k_r.at[2], zdev(d))
                send(kf, kg.at[NZ + z], k_s.at[2], k_r.at[2], zxdev(d))
        if i == 3:
            await_bytes(kg.at[pl.ds(0, 15)], k_r.at[2])
            for n in range(8):
                kgrad_ref[:, 128 * n : 128 * (n + 1)] = (kg[n, 0:9] + kg[NZ + n, 0:9]) * FACTOR

    at_first(hv, 0, 0)
    at_first(hv, 0, 1)
    at_first(hv, 0, 2)
    rs_final(3)
    rs_final(4)
    at_first(hv, 0, 4)
    at_first(hv, 0, 3)
    at_second(hv, 0, 0)
    at_second(hv, 0, 1)
    at_second(hv, 0, 4)
    at_second(hv, 0, 3)
    at_first(av, 1, 4)
    at_second(hv, 0, 2)
    at_first(av, 1, 3)
    at_first(av, 1, 2)
    mgrad_part(0)
    mgrad_part(4)
    sc_own(pm, sbm, qm, finm, 0)
    mgrad_sum(4, 0)
    mgrad_part(3)
    at_second(av, 1, 4)
    mgrad_sum(3, 0)
    at_first(av, 1, 1)
    mgrad_part(2)
    mgrad_sum(3, 1)
    at_second(av, 1, 3)
    mgrad_sum(2, 0)
    at_first(av, 1, 0)
    mgrad_part(1)
    mgrad_sum(2, 1)
    at_second(av, 1, 2)
    result_part(4)
    mgrad_sum(1, 0)
    result_sum(4, 0)
    at_second(av, 1, 1)
    mgrad_sum(1, 1)
    result_part(3)
    result_sum(3, 0)
    at_second(av, 1, 0)
    grad_in(0, 2)
    result_sum(3, 1)
    mg[...] = sc_total(pm, sbm, finm, 0)
    k_stage(0)
    result_part(2)
    k_stage(1)
    result_sum(2, 0)
    result_part(1)
    result_sum(2, 1)
    result_part(0)
    k_stage(2)
    sc_own(pr, sbr, qr, finr, 1)
    result_sum(1, 0)
    k_stage(4)
    grad_in(2, 4)
    result_sum(1, 1)
    grad_in(4, 8)
    grad_out(0, 7)
    k_stage(3)
    result_ref[...] = sc_total(pr, sbr, finr, 1)

    await_bytes(halo.at[pl.ds(0, 2)], halo_s)
    await_bytes(mhalo, mh_s)
    for i in range(2):
        await_bytes(ct.at[pl.ds(0, 992)], ag_s.at[i])
        await_bytes(gp.at[pl.ds(0, 896)], rs_s.at[i])
        await_bytes(hv.at[pl.ds(0, 896)], at_s.at[i])
        await_bytes(pm.at[pl.ds(0, 992)], sc_s.at[i])
    await_bytes(kz, k_s.at[1])
    await_bytes(kg.at[pl.ds(0, 15)], k_s.at[2])


def write_out(*refs):
    copies = [pltpu.make_async_copy(refs[i], refs[5 + i], refs[10].at[i]) for i in range(5)]
    for cp in copies:
        cp.start()
    for cp in copies:
        cp.wait()


def on_device(field, w_in, w_out, taps, cotangent):
    vm, hbm = pl.BlockSpec(memory_space=pltpu.VMEM), pl.BlockSpec(memory_space=pl.ANY)
    dma = pltpu.SemaphoreType.DMA
    shapes = [
        ((COLS, DB), F32), ((COLS, DB), F32), ((9, DB), F32),
        ((DB, FB), F32), ((FB, DB), F32),
    ]
    scratch = [
        pltpu.VMEM((9, DB), F32), pltpu.VMEM((DB, FB), BF16), pltpu.VMEM((FB, DB), BF16),
        pltpu.VMEM((TOKENS, DB), BF16), pltpu.VMEM((TOKENS, DB), BF16),
        pltpu.VMEM((TOKENS, FB), BF16), pltpu.VMEM((TOKENS, FB), BF16),
        pltpu.VMEM((2, 512, CA), BF16), pltpu.VMEM((2, 512, CA), BF16), pltpu.VMEM((2, 384, CA), BF16),
        pltpu.VMEM((2, 768, CB), BF16), pltpu.VMEM((2, 128, CB), BF16), pltpu.VMEM((2, 128, CB), BF16),
        pltpu.VMEM((2, 128, CB), F32),
        pltpu.VMEM((TOKENS, FB), BF16), pltpu.VMEM((TOKENS, FB), BF16),
        pltpu.VMEM((TOKENS, DB), BF16), pltpu.VMEM((TOKENS, DB), BF16),
        pltpu.VMEM((512, DB), BF16), pltpu.VMEM((512, DB), BF16),
        pltpu.VMEM((512, DB), BF16), pltpu.VMEM((512, DB), BF16),
        pltpu.VMEM((512, DB), BF16), pltpu.VMEM((512, DB), BF16),
        pltpu.VMEM((5, 32, DB), BF16), pltpu.VMEM((5, 32, DB), BF16),
        pltpu.VMEM((3, COLS, DB), BF16), pltpu.VMEM((COLS, DB), F32), pltpu.VMEM((2, COLS, DB), F32),
        pltpu.VMEM((8, 16, 128), F32), pltpu.VMEM((8, 16, 128), F32), pltpu.VMEM((7, 16, 128), F32),
        pltpu.VMEM((16, 128), F32), pltpu.VMEM((16, 16, 128), F32),
        dma((5,)), dma, dma, dma((2,)), dma((2, 17)), dma((2, 5)),
        dma((2,)), dma((3, 5)), dma((2,)), dma((2, 5, 2)),
        dma((2,)), dma((2, 5)), dma((2, len(RING))), dma((2,)), dma, dma, dma((3,)), dma((3,)),
    ]
    held = pl.pallas_call(
        kernel,
        out_shape=[pltpu.VMEM(*x) for x in shapes],
        in_specs=[hbm] * 5,
        out_specs=[vm] * 5,
        scratch_shapes=scratch,
        compiler_params=pltpu.CompilerParams(
            collective_id=0, has_side_effects=True, vmem_limit_bytes=48 * 2**20
        ),
        cost_estimate=pl.CostEstimate(flops=6 * 2 * 1024 * 1024 * 896, bytes_accessed=12 * 2**20, transcendentals=0),
        name="block",
    )(field.reshape(COLS, DB), cotangent.reshape(COLS, DB), taps, w_in, w_out)
    result, fgrad, kgrad, grad_in, grad_out = pl.pallas_call(
        write_out,
        out_shape=[jax.ShapeDtypeStruct(*x) for x in shapes],
        in_specs=[hbm] * 5,
        out_specs=[pl.BlockSpec(memory_space=pltpu.HBM)] * 5,
        scratch_shapes=[dma((5,))],
        compiler_params=pltpu.CompilerParams(vmem_limit_bytes=2**20),
        name="write_out",
    )(*held)
    return (result.reshape(1, COLS, DB), fgrad.reshape(1, COLS, DB), grad_in, grad_out, kgrad)


def solution(mesh):
    space = P("space", None, "tensor")
    return jax.shard_map(
        on_device,
        mesh=mesh,
        in_specs=(space, P("tensor", "space"), P("space", "tensor"), P(None, "tensor"), space),
        out_specs=(space, space, P("tensor", "space"), P("space", "tensor"), P(None, "tensor")),
        check_vma=False,
    )
```

```python
import functools
import math

import jax
import jax.numpy as jnp
from jax import lax
from jax.experimental import pallas as pl
from jax.experimental.pallas import tpu as pltpu
from jax.sharding import PartitionSpec as P

MESH = pl.DeviceIdType.MESH
F32, BF16 = jnp.float32, jnp.bfloat16
OFFSETS = [(-1, -1), (-1, 0), (-1, 1), (0, -1), (0, 0), (0, 1), (1, -1), (1, 0), (1, 1)]

NZ, NY, NT = 8, 4, 8
COLS, TOKENS, DB, FB = 32, 1024, 1024, 896
FACTOR = 1.0 / math.sqrt(TOKENS)

ORDER = [0, 1, 7, 2, 6, 3, 5, 4]
POS = {dz: 128 * i for i, dz in enumerate(ORDER)}
CHUNKS = [(0, 128), (128, 256), (384, 256), (640, 256), (896, 128)]
CHUNK_DZ = [[0], [1, 7], [2, 6], [3, 5], [4]]
OWN = [0, 16, 48, 80, 112]
RING = [(3, 0), (5, 1)] + [(dz, xr) for dz in (1, 2, 6, 7) for xr in range(2)]
CA = 512
CB = FB - CA
PA, PB = pl.ds(0, CA), pl.ds(CA, CB)


def gelu_pair(hidden):
    c = math.sqrt(2.0 / math.pi)
    square = hidden * hidden
    th = jnp.tanh(c * (hidden + 0.044715 * (square * hidden)))
    half = 0.5 * (1.0 + th)
    slope = half + 0.5 * hidden * (1.0 - th * th) * (c * (1.0 + (3.0 * 0.044715) * square))
    return hidden * half, slope


def kernel(
    field_hbm, cot_hbm, taps_hbm, wi_hbm, wo_hbm,
    result_ref, fgrad_ref, kgrad_ref, gin, gout,
    taps_ref, wi, wo, ct, mx, gp, hp, xa, ya, yain, ybin, xb, xbin, ownb, av, hv,
    pm, pr, sbm, sbr, qm, qr, rrm, rrr, finm, finr, halo, mg, mhalo,
    kp, kr, kz, kf, kg,
    lsem, halo_s, halo_r, ag_s, ag_r, sib_r, rs_s, rs_r, at_s, at_r,
    sc_s, sc_sib, sc_ring, sc_fin, mh_s, mh_r, k_s, k_r,
):
    s, t = lax.axis_index("space"), lax.axis_index("tensor")
    core, z, xh = s % 2, (s // 2) % NZ, s // (2 * NZ)
    y, xl = t // 2, t % 2

    def zdev(dz):
        return ((xh * NZ + (z + dz) % NZ) * 2 + core, t)

    def ydev(dy):
        return (s, ((y + dy) % NY) * 2 + xl)

    def zxdev(dz):
        return (((1 - xh) * NZ + (z + dz) % NZ) * 2 + core, t)

    xdev = (((1 - xh) * NZ + z) * 2 + core, t)
    ldev = (s, y * 2 + 1 - xl)
    sib = ((xh * NZ + z) * 2 + 1 - core, t)
    nxt, prv = ((s + 1) % 32, t), ((s + 31) % 32, t)

    def send(src, dst, ssem, rsem, dev):
        pltpu.make_async_remote_copy(
            src_ref=src, dst_ref=dst, send_sem=ssem, recv_sem=rsem, device_id=dev, device_id_type=MESH
        ).start()

    def await_bytes(ref, sem):
        pltpu.make_async_copy(ref, ref, sem).wait()

    load_wi = pltpu.make_async_copy(wi_hbm, wi, lsem.at[0])
    load_wo = pltpu.make_async_copy(wo_hbm, wo, lsem.at[1])
    loads = [
        pltpu.make_async_copy(cot_hbm, ct.at[pl.ds(0, 32)], lsem.at[2]),
        pltpu.make_async_copy(field_hbm, halo.at[1], lsem.at[3]),
        pltpu.make_async_copy(taps_hbm, taps_ref, lsem.at[4]),
    ]
    for cp in loads:
        cp.start()
    load_wo.start()
    load_wi.start()

    partners = [ydev(d) for d in range(1, NY)] + [zdev(1), zdev(-1), ldev, xdev, nxt, prv]
    barrier = pltpu.get_barrier_semaphore()
    for dev in partners:
        pl.semaphore_signal(barrier, inc=1, device_id=dev, device_id_type=MESH)
    for cp in loads:
        cp.wait()
    pl.semaphore_wait(barrier, len(partners))

    def ag_begin(buf, i):
        own = buf.at[pl.ds(0, 32)]
        send(own, buf.at[pl.ds(POS[7], 32)], ag_s.at[i], ag_r.at[i, 1], zdev(1))
        send(own, buf.at[pl.ds(POS[1], 32)], ag_s.at[i], ag_r.at[i, 2], zdev(-1))
        send(own, buf.at[pl.ds(32, 32)], ag_s.at[i], ag_r.at[i, 0], xdev)
        send(own, buf.at[pl.ds(64, 32)], ag_s.at[i], sib_r.at[i, 0], sib)

    def ag_cross(buf, i):
        got = buf.at[pl.ds(32, 32)]
        await_bytes(got, ag_r.at[i, 0])
        send(got, buf.at[pl.ds(POS[7] + 32, 32)], ag_s.at[i], ag_r.at[i, 3], zdev(1))
        send(got, buf.at[pl.ds(POS[1] + 32, 32)], ag_s.at[i], ag_r.at[i, 4], zdev(-1))
        send(got, buf.at[pl.ds(96, 32)], ag_s.at[i], sib_r.at[i, 0], sib)

    def ag_step(buf, i, j):
        for xr in range(2):
            for way, (dz, ahead, nz) in enumerate(((NZ - j, 1, NZ - j - 1), (j, -1, j + 1))):
                if j == 4 and way != xr:
                    continue
                piece = buf.at[pl.ds(POS[dz] + 32 * xr, 32)]
                await_bytes(piece, ag_r.at[i, 4 * (j - 1) + 1 + 2 * xr + way])
                if j < 3 or (j == 3 and way == xr):
                    send(
                        piece, buf.at[pl.ds(POS[nz] + 32 * xr, 32)], ag_s.at[i],
                        ag_r.at[i, 4 * j + 1 + 2 * xr + way], zdev(ahead),
                    )
        for dz in CHUNK_DZ[j]:
            send(buf.at[pl.ds(POS[dz], 64)], buf.at[pl.ds(POS[dz] + 64, 64)], ag_s.at[i], sib_r.at[i, j], sib)

    def ag_ready(buf, i, j):
        await_bytes(buf.at[pl.ds(0, CHUNKS[j][1] // 2)], sib_r.at[i, j])

    def mm(src, w, out, chunk, transposed):
        first, length = CHUNKS[chunk]
        left = src.at[pl.ds(first, length)]

        if transposed:
            block = lax.dot_general(left[...], w[...], (((1,), (1,)), ((), ())), preferred_element_type=F32)
        else:
            block = jnp.dot(left[...], w[...], preferred_element_type=F32)
        out[pl.ds(first, length)] = block.astype(BF16)

    def rows_of(start, length, w):
        return pl.ds(pl.multiple_of(start, w), length)

    def rs_first(part, i, c):
        first, w = CHUNKS[c][0], CHUNKS[c][1] // NT
        send(
            part.at[rows_of(first + (1 - xl) * 4 * w, 4 * w, w), PA], xa.at[i, pl.ds(4 * OWN[c], 4 * w)],
            rs_s.at[i], rs_r.at[i, c], ldev,
        )
        for d in range(1, NY):
            to = (y + d) % NY
            send(
                part.at[rows_of(first + to * 2 * w, 2 * w, w), PB],
                ybin.at[i, pl.ds(6 * OWN[c] + (d - 1) * 2 * w, 2 * w)],
                rs_s.at[i], rs_r.at[i, c], ydev(d),
            )

    def rs_second(part, i, c):
        first, w = CHUNKS[c][0], CHUNKS[c][1] // NT
        got = xa.at[i, pl.ds(4 * OWN[c], 4 * w)]
        await_bytes(gp.at[pl.ds(0, 17 * w), pl.ds(0, 256)], rs_r.at[i, c])
        mine = part[rows_of(first + xl * 4 * w, 4 * w, w), PA].astype(F32)
        ya[i, pl.ds(4 * OWN[c], 4 * w)] = (mine + got[...].astype(F32)).astype(BF16)
        for d in range(1, NY):
            to = (y + d) % NY
            send(
                ya.at[i, rows_of(4 * OWN[c] + to * w, w, w)], yain.at[i, pl.ds(3 * OWN[c] + (d - 1) * w, w)],
                rs_s.at[i], rs_r.at[2, c], ydev(d),
            )
        for own in range(2):
            half = xl if own else 1 - xl
            total = part[rows_of(first + (y * 2 + half) * w, w, w), PB].astype(F32)
            for d in range(3):
                total = total + ybin[i, rows_of(6 * OWN[c] + (2 * d + half) * w, w, w)].astype(F32)
            if own:
                ownb[i, pl.ds(OWN[c], w)] = total
            else:
                xb[i, pl.ds(OWN[c], w)] = total.astype(BF16)
                send(
                    xb.at[i, pl.ds(OWN[c], w)], xbin.at[i, pl.ds(OWN[c], w)],
                    rs_s.at[i], rs_r.at[2, c], ldev,
                )

    def rs_final(c):
        first, w = CHUNKS[c][0], CHUNKS[c][1] // NT
        mine = pl.ds(OWN[c], w)
        await_bytes(gp.at[pl.ds(0, 15 * w), pl.ds(0, 256)], rs_r.at[2, c])

        def store(sums, rows, columns):
            act, slope = gelu_pair(sums[1])
            hv[rows, columns] = (sums[0] * slope).astype(BF16)
            av[rows, columns] = act.astype(BF16)

        sums = []
        for i in range(2):
            total = ya[i, rows_of(4 * OWN[c] + y * w, w, w)].astype(F32)
            for d in range(3):
                total = total + yain[i, pl.ds(3 * OWN[c] + d * w, w)].astype(F32)
            sums.append(total)
        store(sums, rows_of(first + (xl * 4 + y) * w, w, w), PA)
        sums = [ownb[i, mine] + xbin[i, mine].astype(F32) for i in range(2)]
        store(sums, rows_of(first + (y * 2 + xl) * w, w, w), PB)

    def at_first(buf, i, c):
        first, w = CHUNKS[c][0], CHUNKS[c][1] // NT
        piece = buf.at[rows_of(first + (xl * 4 + y) * w, w, w), PA]
        for d in range(1, NY):
            send(piece, piece, at_s.at[i], at_r.at[i, c, 0], ydev(d))
        piece = buf.at[rows_of(first + (y * 2 + xl) * w, w, w), PB]
        send(piece, piece, at_s.at[i], at_r.at[i, c, 0], ldev)

    def at_second(buf, i, c):
        first, w = CHUNKS[c][0], CHUNKS[c][1] // NT
        await_bytes(gp.at[pl.ds(0, 5 * w), PB], at_r.at[i, c, 0])
        piece = buf.at[rows_of(first + y * 2 * w, 2 * w, w), PB]
        for d in range(1, NY):
            send(piece, piece, at_s.at[i], at_r.at[i, c, 1], ydev(d))
        piece = buf.at[rows_of(first + xl * 4 * w, 4 * w, w), PA]
        send(piece, piece, at_s.at[i], at_r.at[i, c, 1], ldev)

    def at_wait(buf, i, c):
        first, w = CHUNKS[c][0], CHUNKS[c][1] // NT
        await_bytes(gp.at[pl.ds(0, 17 * w), pl.ds(0, 256)], at_r.at[i, c, 1])

    def grad_tile(left, right, out, n):
        block = lax.dot_general(
            left[:, 128 * n : 128 * (n + 1)], right[...], (((0,), (0,)), ((), ())), preferred_element_type=F32
        )
        out[pl.ds(128 * n, 128)] = block * FACTOR

    def grad_in(lo, hi):
        for n in range(lo, hi):
            grad_tile(mx, hv, gin, n)

    def grad_out(lo, hi):
        for n in range(lo, hi):
            grad_tile(av, ct, gout, n)

    def sc_sibling(part, sb, i, chunk):
        for dz in CHUNK_DZ[chunk]:
            send(part.at[pl.ds(POS[dz] + 64, 64)], sb.at[pl.ds(64 * dz, 64)], sc_s.at[i], sc_sib.at[i, chunk], sib)

    def sc_piece(part, sb, q, rr, fin, i, dz, xr):
        rows = pl.ds(64 * dz + 32 * xr, 32)
        total = part[pl.ds(POS[dz] + 32 * xr, 32)].astype(F32) + sb[rows].astype(F32)
        if (dz, xr) in RING:
            await_bytes(rr.at[rows], sc_ring.at[i, RING.index((dz, xr))])
            total = total + rr[rows].astype(F32)
        q[rows] = total.astype(BF16)
        way = 1 if dz < 4 or (dz == 4 and xr == 0) else -1
        if dz in (1, 7):
            slot = (0 if dz == 1 else 2) + xr
            dev = zxdev(way) if xr else zdev(way)
            send(q.at[rows], fin.at[slot], sc_s.at[i], sc_fin.at[i], dev)
        else:
            to = 64 * (dz - way) + 32 * xr
            send(q.at[rows], rr.at[pl.ds(to, 32)], sc_s.at[i], sc_ring.at[i, RING.index((dz - way, xr))], zdev(way))

    def sc_chunk(part, sb, q, rr, fin, i, chunk, late):
        if not late:
            await_bytes(sb.at[pl.ds(0, CHUNKS[chunk][1] // 2)], sc_sib.at[i, chunk])
        for dz, xr in ((chunk, 1 - late), (NZ - chunk, late)):
            sc_piece(part, sb, q, rr, fin, i, dz, xr)

    def sc_own(part, sb, q, fin, i):
        await_bytes(sb.at[pl.ds(0, 64)], sc_sib.at[i, 0])
        q[pl.ds(32, 32)] = (part[pl.ds(32, 32)].astype(F32) + sb[pl.ds(32, 32)].astype(F32)).astype(BF16)
        send(q.at[pl.ds(32, 32)], fin.at[4], sc_s.at[i], sc_fin.at[i], xdev)

    def sc_total(part, sb, fin, i):
        total = part[pl.ds(0, 32)].astype(F32) + sb[pl.ds(0, 32)].astype(F32)
        await_bytes(fin, sc_fin.at[i])
        for slot in range(5):
            total = total + fin[slot].astype(F32)
        return total

    send(halo.at[1], halo.at[0], halo_s, halo_r, nxt)
    send(halo.at[1], halo.at[2], halo_s, halo_r, prv)
    ag_begin(ct, 0)
    await_bytes(halo.at[pl.ds(0, 2)], halo_r)

    def conv_tile(i, carry):
        lanes = pl.ds(pl.multiple_of(i * 128, 128), 128)
        rows = [halo[r, :, lanes].astype(F32) for r in range(3)]
        total = jnp.zeros((COLS, 128), F32)
        for k, (dr, dc) in enumerate(OFFSETS):
            moved = rows[1 + dr] if dc == 0 else pltpu.roll(rows[1 + dr], (-dc) % COLS, 0)
            total = total + taps_ref[k : k + 1, lanes] * moved
        mx[pl.ds(0, 32), lanes] = (rows[1] + total).astype(BF16)
        return carry

    lax.fori_loop(0, 8, conv_tile, 0)
    ag_cross(ct, 0)
    ag_begin(mx, 1)
    load_wo.wait()
    def cot_chunk(c):
        if c > 0:
            ag_step(ct, 0, c)
        ag_ready(ct, 0, c)
        mm(ct, wo, gp, c, True)
        rs_first(gp, 0, c)

    def mixed_chunk(c):
        if c > 0:
            ag_step(mx, 1, c)
        else:
            ag_cross(mx, 1)
            load_wi.wait()
        ag_ready(mx, 1, c)
        mm(mx, wi, hp, c, False)
        rs_first(hp, 1, c)

    cot_chunk(0)
    for c in range(5):
        if c < 4:
            cot_chunk(c + 1)
        mixed_chunk(c)
        if c > 0:
            rs_second(gp, 0, c - 1)
            rs_second(hp, 1, c - 1)
        if c > 1:
            rs_final(c - 2)
    rs_second(gp, 0, 4)
    rs_second(hp, 1, 4)

    def mgrad_part(c):
        at_wait(hv, 0, c)
        mm(hv, wi, pm, c, True)
        sc_sibling(pm, sbm, 0, c)

    def result_part(c):
        at_wait(av, 1, c)
        mm(av, wo, pr, c, False)
        sc_sibling(pr, sbr, 1, c)

    def mgrad_sum(c, late):
        sc_chunk(pm, sbm, qm, rrm, finm, 0, c, late)

    def result_sum(c, late):
        sc_chunk(pr, sbr, qr, rrr, finr, 1, c, late)

    def k_stage(i):
        if i == 0:
            send(mg, mhalo.at[0], mh_s, mh_r, nxt)
            send(mg, mhalo.at[1], mh_s, mh_r, prv)

            def kgrad_tile(n, carry):
                lanes = pl.ds(pl.multiple_of(n * 128, 128), 128)
                grad = mg[:, lanes]
                rows = [halo[r, :, lanes].astype(F32) for r in range(3)]
                sums = []
                for dr, dc in OFFSETS:
                    moved = rows[1 + dr] if dc == 0 else pltpu.roll(rows[1 + dr], (-dc) % COLS, 0)
                    sums.append(jnp.sum(grad * moved, axis=0, keepdims=True))
                kp[n] = jnp.concatenate(sums + [jnp.zeros((7, 128), F32)], axis=0)
                return carry

            lax.fori_loop(0, 8, kgrad_tile, 0)
            send(kp, kr, k_s.at[0], k_r.at[0], sib)
        if i == 1:
            await_bytes(kr, k_r.at[0])
            await_bytes(kp, k_s.at[0])
            kp[...] = kp[...] + kr[...]
            for d in range(1, NZ):
                send(kp.at[(z + d) % NZ], kz.at[d - 1], k_s.at[1], k_r.at[1], zdev(d))
        if i == 4:
            await_bytes(mhalo, mh_r)

            def fgrad_tile(n, carry):
                lanes = pl.ds(pl.multiple_of(n * 128, 128), 128)
                rows = [mhalo[0, :, lanes], mg[:, lanes], mhalo[1, :, lanes]]
                total = rows[1]
                for k, (dr, dc) in enumerate(OFFSETS):
                    moved = rows[1 - dr] if dc == 0 else pltpu.roll(rows[1 - dr], dc % COLS, 0)
                    total = total + taps_ref[k : k + 1, lanes] * moved
                fgrad_ref[:, lanes] = total
                return carry

            lax.fori_loop(0, 8, fgrad_tile, 0)
        if i == 2:
            await_bytes(kz, k_r.at[1])
            total = kp[z]
            for n in range(7):
                total = total + kz[n]
            kf[...] = total
            kg[z] = total
            for d in range(NZ):
                if d > 0:
                    send(kf, kg.at[z], k_s.at[2], k_r.at[2], zdev(d))
                send(kf, kg.at[NZ + z], k_s.at[2], k_r.at[2], zxdev(d))
        if i == 3:
            await_bytes(kg.at[pl.ds(0, 15)], k_r.at[2])
            for n in range(8):
                kgrad_ref[:, 128 * n : 128 * (n + 1)] = (kg[n, 0:9] + kg[NZ + n, 0:9]) * FACTOR

    at_first(hv, 0, 0)
    at_first(hv, 0, 1)
    at_first(hv, 0, 2)
    rs_final(3)
    rs_final(4)
    at_first(hv, 0, 4)
    at_first(hv, 0, 3)
    at_second(hv, 0, 0)
    at_second(hv, 0, 1)
    at_second(hv, 0, 4)
    at_second(hv, 0, 3)
    at_first(av, 1, 4)
    at_second(hv, 0, 2)
    at_first(av, 1, 3)
    at_first(av, 1, 2)
    at_first(av, 1, 1)
    at_first(av, 1, 0)
    mgrad_part(0)
    mgrad_part(4)
    sc_own(pm, sbm, qm, finm, 0)
    mgrad_sum(4, 0)
    mgrad_part(3)
    at_second(av, 1, 4)
    mgrad_sum(3, 0)
    mgrad_part(2)
    mgrad_sum(3, 1)
    at_second(av, 1, 3)
    mgrad_sum(2, 0)
    at_second(av, 1, 2)
    mgrad_part(1)
    mgrad_sum(2, 1)
    result_part(4)
    at_second(av, 1, 1)
    mgrad_sum(1, 0)
    result_sum(4, 0)
    at_second(av, 1, 0)
    mgrad_sum(1, 1)
    result_part(3)
    result_sum(3, 0)
    grad_in(0, 2)
    result_sum(3, 1)
    mg[...] = sc_total(pm, sbm, finm, 0)
    k_stage(0)
    result_part(2)
    k_stage(1)
    result_sum(2, 0)
    result_part(1)
    result_sum(2, 1)
    result_part(0)
    grad_in(2, 4)
    sc_own(pr, sbr, qr, finr, 1)
    grad_in(4, 6)
    k_stage(2)
    result_sum(1, 0)
    k_stage(4)
    result_sum(1, 1)
    grad_in(6, 8)
    grad_out(0, 7)
    k_stage(3)
    result_ref[...] = sc_total(pr, sbr, finr, 1)

    await_bytes(halo.at[pl.ds(0, 2)], halo_s)
    await_bytes(mhalo, mh_s)
    for i in range(2):
        await_bytes(ct.at[pl.ds(0, 992)], ag_s.at[i])
        await_bytes(gp.at[pl.ds(0, 896)], rs_s.at[i])
        await_bytes(hv.at[pl.ds(0, 896)], at_s.at[i])
        await_bytes(pm.at[pl.ds(0, 992)], sc_s.at[i])
    await_bytes(kz, k_s.at[1])
    await_bytes(kg.at[pl.ds(0, 15)], k_s.at[2])


def write_out(*refs):
    copies = [pltpu.make_async_copy(refs[i], refs[5 + i], refs[10].at[i]) for i in range(5)]
    for cp in copies:
        cp.start()
    for cp in copies:
        cp.wait()


def on_device(field, w_in, w_out, taps, cotangent):
    vm, hbm = pl.BlockSpec(memory_space=pltpu.VMEM), pl.BlockSpec(memory_space=pl.ANY)
    dma = pltpu.SemaphoreType.DMA
    shapes = [
        ((COLS, DB), F32), ((COLS, DB), F32), ((9, DB), F32),
        ((DB, FB), F32), ((FB, DB), F32),
    ]
    scratch = [
        pltpu.VMEM((9, DB), F32), pltpu.VMEM((DB, FB), BF16), pltpu.VMEM((FB, DB), BF16),
        pltpu.VMEM((TOKENS, DB), BF16), pltpu.VMEM((TOKENS, DB), BF16),
        pltpu.VMEM((TOKENS, FB), BF16), pltpu.VMEM((TOKENS, FB), BF16),
        pltpu.VMEM((2, 512, CA), BF16), pltpu.VMEM((2, 512, CA), BF16), pltpu.VMEM((2, 384, CA), BF16),
        pltpu.VMEM((2, 768, CB), BF16), pltpu.VMEM((2, 128, CB), BF16), pltpu.VMEM((2, 128, CB), BF16),
        pltpu.VMEM((2, 128, CB), F32),
        pltpu.VMEM((TOKENS, FB), BF16), pltpu.VMEM((TOKENS, FB), BF16),
        pltpu.VMEM((TOKENS, DB), BF16), pltpu.VMEM((TOKENS, DB), BF16),
        pltpu.VMEM((512, DB), BF16), pltpu.VMEM((512, DB), BF16),
        pltpu.VMEM((512, DB), BF16), pltpu.VMEM((512, DB), BF16),
        pltpu.VMEM((512, DB), BF16), pltpu.VMEM((512, DB), BF16),
        pltpu.VMEM((5, 32, DB), BF16), pltpu.VMEM((5, 32, DB), BF16),
        pltpu.VMEM((3, COLS, DB), BF16), pltpu.VMEM((COLS, DB), F32), pltpu.VMEM((2, COLS, DB), F32),
        pltpu.VMEM((8, 16, 128), F32), pltpu.VMEM((8, 16, 128), F32), pltpu.VMEM((7, 16, 128), F32),
        pltpu.VMEM((16, 128), F32), pltpu.VMEM((16, 16, 128), F32),
        dma((5,)), dma, dma, dma((2,)), dma((2, 17)), dma((2, 5)),
        dma((2,)), dma((3, 5)), dma((2,)), dma((2, 5, 2)),
        dma((2,)), dma((2, 5)), dma((2, len(RING))), dma((2,)), dma, dma, dma((3,)), dma((3,)),
    ]
    held = pl.pallas_call(
        kernel,
        out_shape=[pltpu.VMEM(*x) for x in shapes],
        in_specs=[hbm] * 5,
        out_specs=[vm] * 5,
        scratch_shapes=scratch,
        compiler_params=pltpu.CompilerParams(
            collective_id=0, has_side_effects=True, vmem_limit_bytes=48 * 2**20
        ),
        cost_estimate=pl.CostEstimate(flops=6 * 2 * 1024 * 1024 * 896, bytes_accessed=12 * 2**20, transcendentals=0),
        name="block",
    )(field.reshape(COLS, DB), cotangent.reshape(COLS, DB), taps, w_in, w_out)
    result, fgrad, kgrad, grad_in, grad_out = pl.pallas_call(
        write_out,
        out_shape=[jax.ShapeDtypeStruct(*x) for x in shapes],
        in_specs=[hbm] * 5,
        out_specs=[pl.BlockSpec(memory_space=pltpu.HBM)] * 5,
        scratch_shapes=[dma((5,))],
        compiler_params=pltpu.CompilerParams(vmem_limit_bytes=2**20),
        name="write_out",
    )(*held)
    return (result.reshape(1, COLS, DB), fgrad.reshape(1, COLS, DB), grad_in, grad_out, kgrad)


def solution(mesh):
    space = P("space", None, "tensor")
    return jax.shard_map(
        on_device,
        mesh=mesh,
        in_specs=(space, P("tensor", "space"), P("space", "tensor"), P(None, "tensor"), space),
        out_specs=(space, space, P("tensor", "space"), P("space", "tensor"), P(None, "tensor")),
        check_vma=False,
    )
```

```python
import functools
import math

import jax
import jax.numpy as jnp
from jax import lax
from jax.experimental import pallas as pl
from jax.experimental.pallas import tpu as pltpu
from jax.sharding import PartitionSpec as P

MESH = pl.DeviceIdType.MESH
F32, BF16 = jnp.float32, jnp.bfloat16
OFFSETS = [(-1, -1), (-1, 0), (-1, 1), (0, -1), (0, 0), (0, 1), (1, -1), (1, 0), (1, 1)]

NZ, NY, NT = 8, 4, 8
COLS, TOKENS, DB, FB = 32, 1024, 1024, 896
FACTOR = 1.0 / math.sqrt(TOKENS)

ORDER = [0, 1, 7, 2, 6, 3, 5, 4]
POS = {dz: 128 * i for i, dz in enumerate(ORDER)}
CHUNKS = [(0, 128), (128, 256), (384, 256), (640, 256), (896, 128)]
CHUNK_DZ = [[0], [1, 7], [2, 6], [3, 5], [4]]
OWN = [0, 16, 48, 80, 112]
RING = [(3, 0), (5, 1), (2, 1), (6, 0), (2, 0), (6, 1), (1, 1), (7, 0), (1, 0), (7, 1)]
CA = 512
CB = FB - CA
PA, PB = pl.ds(0, CA), pl.ds(CA, CB)


def gelu_pair(hidden):
    c = math.sqrt(2.0 / math.pi)
    square = hidden * hidden
    th = jnp.tanh(c * (hidden + 0.044715 * (square * hidden)))
    half = 0.5 * (1.0 + th)
    slope = half + 0.5 * hidden * (1.0 - th * th) * (c * (1.0 + (3.0 * 0.044715) * square))
    return hidden * half, slope


def kernel(
    field_hbm, cot_hbm, taps_hbm, wi_hbm, wo_hbm,
    result_ref, fgrad_ref, kgrad_ref, gin, gout,
    taps_ref, wi, wo, ct, mx, gp, hp, xa, ya, yain, ybin, xb, xbin, ownb, av, hv,
    pm, pr, sbm, sbr, qm, qr, rrm, rrr, finm, finr, halo, mg, mhalo,
    kp, kr, kz, kf, kg,
    lsem, halo_s, halo_r, ag_s, ag_r, sib_r, rs_s, rs_r, at_s, at_r,
    sc_s, sc_sib, sc_ring, sc_fin, mh_s, mh_r, k_s, k_r,
):
    s, t = lax.axis_index("space"), lax.axis_index("tensor")
    core, z, xh = s % 2, (s // 2) % NZ, s // (2 * NZ)
    y, xl = t // 2, t % 2

    def zdev(dz):
        return ((xh * NZ + (z + dz) % NZ) * 2 + core, t)

    def ydev(dy):
        return (s, ((y + dy) % NY) * 2 + xl)

    def zxdev(dz):
        return (((1 - xh) * NZ + (z + dz) % NZ) * 2 + core, t)

    xdev = (((1 - xh) * NZ + z) * 2 + core, t)
    ldev = (s, y * 2 + 1 - xl)
    sib = ((xh * NZ + z) * 2 + 1 - core, t)
    nxt, prv = ((s + 1) % 32, t), ((s + 31) % 32, t)

    def send(src, dst, ssem, rsem, dev):
        pltpu.make_async_remote_copy(
            src_ref=src, dst_ref=dst, send_sem=ssem, recv_sem=rsem, device_id=dev, device_id_type=MESH
        ).start()

    def await_bytes(ref, sem):
        pltpu.make_async_copy(ref, ref, sem).wait()

    load_wi = pltpu.make_async_copy(wi_hbm, wi, lsem.at[0])
    load_wo = pltpu.make_async_copy(wo_hbm, wo, lsem.at[1])
    loads = [
        pltpu.make_async_copy(cot_hbm, ct.at[pl.ds(0, 32)], lsem.at[2]),
        pltpu.make_async_copy(field_hbm, halo.at[1], lsem.at[3]),
        pltpu.make_async_copy(taps_hbm, taps_ref, lsem.at[4]),
    ]
    for cp in loads:
        cp.start()
    load_wo.start()
    load_wi.start()

    partners = [ydev(d) for d in range(1, NY)] + [zdev(1), zdev(-1), ldev, xdev, nxt, prv]
    barrier = pltpu.get_barrier_semaphore()
    for dev in partners:
        pl.semaphore_signal(barrier, inc=1, device_id=dev, device_id_type=MESH)
    for cp in loads:
        cp.wait()
    pl.semaphore_wait(barrier, len(partners))

    def ag_begin(buf, i):
        own = buf.at[pl.ds(0, 32)]
        send(own, buf.at[pl.ds(POS[7], 32)], ag_s.at[i], ag_r.at[i, 1], zdev(1))
        send(own, buf.at[pl.ds(POS[1], 32)], ag_s.at[i], ag_r.at[i, 1], zdev(-1))
        send(own, buf.at[pl.ds(32, 32)], ag_s.at[i], ag_r.at[i, 0], xdev)
        send(own, buf.at[pl.ds(64, 32)], ag_s.at[i], sib_r.at[i, 0], sib)

    def ag_cross(buf, i):
        got = buf.at[pl.ds(32, 32)]
        await_bytes(got, ag_r.at[i, 0])
        send(got, buf.at[pl.ds(POS[7] + 32, 32)], ag_s.at[i], ag_r.at[i, 2], zdev(1))
        send(got, buf.at[pl.ds(POS[1] + 32, 32)], ag_s.at[i], ag_r.at[i, 2], zdev(-1))
        send(got, buf.at[pl.ds(96, 32)], ag_s.at[i], sib_r.at[i, 0], sib)

    def ag_step(buf, i, j):
        for xr in range(2 if j < 4 else 1):
            await_bytes(buf.at[pl.ds(POS[j], 64)], ag_r.at[i, 2 * j - 1 + xr])
            for way, (dz, ahead, nz) in enumerate(((NZ - j, 1, NZ - j - 1), (j, -1, j + 1))):
                if j < 3 or (j == 3 and way == xr):
                    send(
                        buf.at[pl.ds(POS[dz] + 32 * xr, 32)], buf.at[pl.ds(POS[nz] + 32 * xr, 32)], ag_s.at[i],
                        ag_r.at[i, 2 * j + 1 + xr if j < 3 else 7], zdev(ahead),
                    )
        for dz in CHUNK_DZ[j]:
            send(buf.at[pl.ds(POS[dz], 64)], buf.at[pl.ds(POS[dz] + 64, 64)], ag_s.at[i], sib_r.at[i, j], sib)

    def ag_ready(buf, i, j):
        await_bytes(buf.at[pl.ds(0, CHUNKS[j][1] // 2)], sib_r.at[i, j])

    def mm(src, w, out, chunk, transposed):
        first, length = CHUNKS[chunk]
        left = src.at[pl.ds(first, length)]

        if transposed:
            block = lax.dot_general(left[...], w[...], (((1,), (1,)), ((), ())), preferred_element_type=F32)
        else:
            block = jnp.dot(left[...], w[...], preferred_element_type=F32)
        out[pl.ds(first, length)] = block.astype(BF16)

    def rows_of(start, length, w):
        return pl.ds(pl.multiple_of(start, w), length)

    def rs_first(part, i, c):
        first, w = CHUNKS[c][0], CHUNKS[c][1] // NT
        send(
            part.at[rows_of(first + (1 - xl) * 4 * w, 4 * w, w), PA], xa.at[i, pl.ds(4 * OWN[c], 4 * w)],
            rs_s.at[i], rs_r.at[i, c], ldev,
        )
        for d in range(1, NY):
            to = (y + d) % NY
            send(
                part.at[rows_of(first + to * 2 * w, 2 * w, w), PB],
                ybin.at[i, pl.ds(6 * OWN[c] + (d - 1) * 2 * w, 2 * w)],
                rs_s.at[i], rs_r.at[i, c], ydev(d),
            )

    def rs_second(part, i, c):
        first, w = CHUNKS[c][0], CHUNKS[c][1] // NT
        got = xa.at[i, pl.ds(4 * OWN[c], 4 * w)]
        await_bytes(gp.at[pl.ds(0, 17 * w), pl.ds(0, 256)], rs_r.at[i, c])
        mine = part[rows_of(first + xl * 4 * w, 4 * w, w), PA].astype(F32)
        ya[i, pl.ds(4 * OWN[c], 4 * w)] = (mine + got[...].astype(F32)).astype(BF16)
        for d in range(1, NY):
            to = (y + d) % NY
            send(
                ya.at[i, rows_of(4 * OWN[c] + to * w, w, w)], yain.at[i, pl.ds(3 * OWN[c] + (d - 1) * w, w)],
                rs_s.at[i], rs_r.at[2, c], ydev(d),
            )
        for own in range(2):
            half = xl if own else 1 - xl
            total = part[rows_of(first + (y * 2 + half) * w, w, w), PB].astype(F32)
            for d in range(3):
                total = total + ybin[i, rows_of(6 * OWN[c] + (2 * d + half) * w, w, w)].astype(F32)
            if own:
                ownb[i, pl.ds(OWN[c], w)] = total
            else:
                xb[i, pl.ds(OWN[c], w)] = total.astype(BF16)
                send(
                    xb.at[i, pl.ds(OWN[c], w)], xbin.at[i, pl.ds(OWN[c], w)],
                    rs_s.at[i], rs_r.at[2, c], ldev,
                )

    def rs_final(c):
        first, w = CHUNKS[c][0], CHUNKS[c][1] // NT
        mine = pl.ds(OWN[c], w)
        await_bytes(gp.at[pl.ds(0, 15 * w), pl.ds(0, 256)], rs_r.at[2, c])

        def store(sums, rows, columns):
            act, slope = gelu_pair(sums[1])
            hv[rows, columns] = (sums[0] * slope).astype(BF16)
            av[rows, columns] = act.astype(BF16)

        sums = []
        for i in range(2):
            total = ya[i, rows_of(4 * OWN[c] + y * w, w, w)].astype(F32)
            for d in range(3):
                total = total + yain[i, pl.ds(3 * OWN[c] + d * w, w)].astype(F32)
            sums.append(total)
        store(sums, rows_of(first + (xl * 4 + y) * w, w, w), PA)
        sums = [ownb[i, mine] + xbin[i, mine].astype(F32) for i in range(2)]
        store(sums, rows_of(first + (y * 2 + xl) * w, w, w), PB)

    def at_first(buf, i, c):
        first, w = CHUNKS[c][0], CHUNKS[c][1] // NT
        piece = buf.at[rows_of(first + (xl * 4 + y) * w, w, w), PA]
        for d in range(1, NY):
            send(piece, piece, at_s.at[i], at_r.at[i, c, 0], ydev(d))
        piece = buf.at[rows_of(first + (y * 2 + xl) * w, w, w), PB]
        send(piece, piece, at_s.at[i], at_r.at[i, c, 0], ldev)

    def at_second(buf, i, c):
        first, w = CHUNKS[c][0], CHUNKS[c][1] // NT
        await_bytes(gp.at[pl.ds(0, 5 * w), PB], at_r.at[i, c, 0])
        piece = buf.at[rows_of(first + y * 2 * w, 2 * w, w), PB]
        for d in range(1, NY):
            send(piece, piece, at_s.at[i], at_r.at[i, c, 1], ydev(d))
        piece = buf.at[rows_of(first + xl * 4 * w, 4 * w, w), PA]
        send(piece, piece, at_s.at[i], at_r.at[i, c, 1], ldev)

    def at_wait(buf, i, c):
        first, w = CHUNKS[c][0], CHUNKS[c][1] // NT
        await_bytes(gp.at[pl.ds(0, 17 * w), pl.ds(0, 256)], at_r.at[i, c, 1])

    def grad_tile(left, right, out, n):
        block = lax.dot_general(
            left[:, 128 * n : 128 * (n + 1)], right[...], (((0,), (0,)), ((), ())), preferred_element_type=F32
        )
        out[pl.ds(128 * n, 128)] = block * FACTOR

    def grad_in(lo, hi):
        for n in range(lo, hi):
            grad_tile(mx, hv, gin, n)

    def grad_out(lo, hi):
        for n in range(lo, hi):
            grad_tile(av, ct, gout, n)

    def sc_sibling(part, sb, i, chunk):
        for dz in CHUNK_DZ[chunk]:
            send(part.at[pl.ds(POS[dz] + 64, 64)], sb.at[pl.ds(64 * dz, 64)], sc_s.at[i], sc_sib.at[i, chunk], sib)

    def sc_piece(part, sb, q, rr, fin, i, dz, xr):
        rows = pl.ds(64 * dz + 32 * xr, 32)
        total = part[pl.ds(POS[dz] + 32 * xr, 32)].astype(F32) + sb[rows].astype(F32)
        if (dz, xr) in RING:
            total = total + rr[rows].astype(F32)
        q[rows] = total.astype(BF16)
        way = 1 if dz < 4 or (dz == 4 and xr == 0) else -1
        if dz in (1, 7):
            slot = (0 if dz == 1 else 2) + xr
            dev = zxdev(way) if xr else zdev(way)
            send(q.at[rows], fin.at[slot], sc_s.at[i], sc_fin.at[i], dev)
        else:
            to = 64 * (dz - way) + 32 * xr
            send(q.at[rows], rr.at[pl.ds(to, 32)], sc_s.at[i], sc_ring.at[i, RING.index((dz - way, xr)) // 2], zdev(way))

    def sc_chunk(part, sb, q, rr, fin, i, chunk, late):
        if not late:
            await_bytes(sb.at[pl.ds(0, CHUNKS[chunk][1] // 2)], sc_sib.at[i, chunk])
        if (chunk, 1 - late) in RING:
            await_bytes(rr.at[pl.ds(0, 64)], sc_ring.at[i, RING.index((chunk, 1 - late)) // 2])
        for dz, xr in ((chunk, 1 - late), (NZ - chunk, late)):
            sc_piece(part, sb, q, rr, fin, i, dz, xr)

    def sc_own(part, sb, q, fin, i):
        await_bytes(sb.at[pl.ds(0, 64)], sc_sib.at[i, 0])
        q[pl.ds(32, 32)] = (part[pl.ds(32, 32)].astype(F32) + sb[pl.ds(32, 32)].astype(F32)).astype(BF16)
        send(q.at[pl.ds(32, 32)], fin.at[4], sc_s.at[i], sc_fin.at[i], xdev)

    def sc_total(part, sb, fin, i):
        total = part[pl.ds(0, 32)].astype(F32) + sb[pl.ds(0, 32)].astype(F32)
        await_bytes(fin, sc_fin.at[i])
        for slot in range(5):
            total = total + fin[slot].astype(F32)
        return total

    send(halo.at[1], halo.at[0], halo_s, halo_r, nxt)
    send(halo.at[1], halo.at[2], halo_s, halo_r, prv)
    ag_begin(ct, 0)
    await_bytes(halo.at[pl.ds(0, 2)], halo_r)

    def conv_tile(i, carry):
        lanes = pl.ds(pl.multiple_of(i * 128, 128), 128)
        rows = [halo[r, :, lanes].astype(F32) for r in range(3)]
        total = jnp.zeros((COLS, 128), F32)
        for k, (dr, dc) in enumerate(OFFSETS):
            moved = rows[1 + dr] if dc == 0 else pltpu.roll(rows[1 + dr], (-dc) % COLS, 0)
            total = total + taps_ref[k : k + 1, lanes] * moved
        mx[pl.ds(0, 32), lanes] = (rows[1] + total).astype(BF16)
        return carry

    lax.fori_loop(0, 8, conv_tile, 0)
    ag_begin(mx, 1)
    ag_cross(ct, 0)
    load_wo.wait()
    def cot_chunk(c):
        if c > 0:
            ag_step(ct, 0, c)
        ag_ready(ct, 0, c)
        mm(ct, wo, gp, c, True)
        rs_first(gp, 0, c)

    def mixed_chunk(c):
        if c > 0:
            ag_step(mx, 1, c)
        else:
            ag_cross(mx, 1)
            load_wi.wait()
        ag_ready(mx, 1, c)
        mm(mx, wi, hp, c, False)
        rs_first(hp, 1, c)

    cot_chunk(0)
    for c in range(5):
        if c < 4:
            cot_chunk(c + 1)
        mixed_chunk(c)
        rs_second(gp, 0, c)
        if c > 0:
            rs_second(hp, 1, c - 1)
    rs_second(hp, 1, 4)

    def mgrad_part(c):
        at_wait(hv, 0, c)
        mm(hv, wi, pm, c, True)
        sc_sibling(pm, sbm, 0, c)

    def result_part(c):
        at_wait(av, 1, c)
        mm(av, wo, pr, c, False)
        sc_sibling(pr, sbr, 1, c)

    def mgrad_sum(c, late):
        sc_chunk(pm, sbm, qm, rrm, finm, 0, c, late)

    def result_sum(c, late):
        sc_chunk(pr, sbr, qr, rrr, finr, 1, c, late)

    def k_stage(i):
        if i == 0:
            send(mg, mhalo.at[0], mh_s, mh_r, nxt)
            send(mg, mhalo.at[1], mh_s, mh_r, prv)

            def kgrad_tile(n, carry):
                lanes = pl.ds(pl.multiple_of(n * 128, 128), 128)
                grad = mg[:, lanes]
                rows = [halo[r, :, lanes].astype(F32) for r in range(3)]
                sums = []
                for dr, dc in OFFSETS:
                    moved = rows[1 + dr] if dc == 0 else pltpu.roll(rows[1 + dr], (-dc) % COLS, 0)
                    sums.append(jnp.sum(grad * moved, axis=0, keepdims=True))
                kp[n] = jnp.concatenate(sums + [jnp.zeros((7, 128), F32)], axis=0)
                return carry

            lax.fori_loop(0, 8, kgrad_tile, 0)
            send(kp, kr, k_s.at[0], k_r.at[0], sib)
        if i == 1:
            await_bytes(kr, k_r.at[0])
            await_bytes(kp, k_s.at[0])
            kp[...] = kp[...] + kr[...]
            for d in range(1, NZ):
                send(kp.at[(z + d) % NZ], kz.at[d - 1], k_s.at[1], k_r.at[1], zdev(d))
        if i == 4:
            await_bytes(mhalo, mh_r)

            def fgrad_tile(n, carry):
                lanes = pl.ds(pl.multiple_of(n * 128, 128), 128)
                rows = [mhalo[0, :, lanes], mg[:, lanes], mhalo[1, :, lanes]]
                total = rows[1]
                for k, (dr, dc) in enumerate(OFFSETS):
                    moved = rows[1 - dr] if dc == 0 else pltpu.roll(rows[1 - dr], dc % COLS, 0)
                    total = total + taps_ref[k : k + 1, lanes] * moved
                fgrad_ref[:, lanes] = total
                return carry

            lax.fori_loop(0, 8, fgrad_tile, 0)
        if i == 2:
            await_bytes(kz, k_r.at[1])
            total = kp[z]
            for n in range(7):
                total = total + kz[n]
            kf[...] = total
            kg[z] = total
            for d in range(NZ):
                if d > 0:
                    send(kf, kg.at[z], k_s.at[2], k_r.at[2], zdev(d))
                send(kf, kg.at[NZ + z], k_s.at[2], k_r.at[2], zxdev(d))
        if i == 3:
            await_bytes(kg.at[pl.ds(0, 15)], k_r.at[2])
            for n in range(8):
                kgrad_ref[:, 128 * n : 128 * (n + 1)] = (kg[n, 0:9] + kg[NZ + n, 0:9]) * FACTOR

    for c in range(3):
        rs_final(c)
        at_first(hv, 0, c)
    rs_final(3)
    rs_final(4)
    at_first(hv, 0, 4)
    at_first(hv, 0, 3)
    at_second(hv, 0, 0)
    at_second(hv, 0, 1)
    at_second(hv, 0, 4)
    at_second(hv, 0, 3)
    at_first(av, 1, 4)
    at_second(hv, 0, 2)
    at_first(av, 1, 3)
    at_first(av, 1, 2)
    at_first(av, 1, 1)
    at_first(av, 1, 0)
    mgrad_part(0)
    mgrad_part(4)
    sc_own(pm, sbm, qm, finm, 0)
    mgrad_sum(4, 0)
    mgrad_part(3)
    at_second(av, 1, 4)
    mgrad_sum(3, 0)
    mgrad_part(2)
    mgrad_sum(3, 1)
    at_second(av, 1, 3)
    mgrad_sum(2, 0)
    at_second(av, 1, 2)
    mgrad_part(1)
    mgrad_sum(2, 1)
    result_part(4)
    mgrad_sum(1, 0)
    at_second(av, 1, 1)
    result_sum(4, 0)
    mgrad_sum(1, 1)
    at_second(av, 1, 0)
    result_part(3)
    result_sum(3, 0)
    grad_in(0, 2)
    result_sum(3, 1)
    mg[...] = sc_total(pm, sbm, finm, 0)
    k_stage(0)
    result_part(2)
    k_stage(1)
    result_sum(2, 0)
    result_part(1)
    result_sum(2, 1)
    result_part(0)
    grad_in(2, 4)
    sc_own(pr, sbr, qr, finr, 1)
    grad_in(4, 6)
    k_stage(2)
    result_sum(1, 0)
    result_sum(1, 1)
    grad_in(6, 8)
    grad_out(0, 7)
    k_stage(4)
    k_stage(3)
    result_ref[...] = sc_total(pr, sbr, finr, 1)

    await_bytes(halo.at[pl.ds(0, 2)], halo_s)
    await_bytes(mhalo, mh_s)
    for i in range(2):
        await_bytes(ct.at[pl.ds(0, 992)], ag_s.at[i])
        await_bytes(gp.at[pl.ds(0, 896)], rs_s.at[i])
        await_bytes(hv.at[pl.ds(0, 896)], at_s.at[i])
        await_bytes(pm.at[pl.ds(0, 992)], sc_s.at[i])
    await_bytes(kz, k_s.at[1])
    await_bytes(kg.at[pl.ds(0, 15)], k_s.at[2])


def write_out(*refs):
    copies = [pltpu.make_async_copy(refs[i], refs[5 + i], refs[10].at[i]) for i in range(5)]
    for cp in copies:
        cp.start()
    for cp in copies:
        cp.wait()


def on_device(field, w_in, w_out, taps, cotangent):
    vm, hbm = pl.BlockSpec(memory_space=pltpu.VMEM), pl.BlockSpec(memory_space=pl.ANY)
    dma = pltpu.SemaphoreType.DMA
    shapes = [
        ((COLS, DB), F32), ((COLS, DB), F32), ((9, DB), F32),
        ((DB, FB), F32), ((FB, DB), F32),
    ]
    scratch = [
        pltpu.VMEM((9, DB), F32), pltpu.VMEM((DB, FB), BF16), pltpu.VMEM((FB, DB), BF16),
        pltpu.VMEM((TOKENS, DB), BF16), pltpu.VMEM((TOKENS, DB), BF16),
        pltpu.VMEM((TOKENS, FB), BF16), pltpu.VMEM((TOKENS, FB), BF16),
        pltpu.VMEM((2, 512, CA), BF16), pltpu.VMEM((2, 512, CA), BF16), pltpu.VMEM((2, 384, CA), BF16),
        pltpu.VMEM((2, 768, CB), BF16), pltpu.VMEM((2, 128, CB), BF16), pltpu.VMEM((2, 128, CB), BF16),
        pltpu.VMEM((2, 128, CB), F32),
        pltpu.VMEM((TOKENS, FB), BF16), pltpu.VMEM((TOKENS, FB), BF16),
        pltpu.VMEM((TOKENS, DB), BF16), pltpu.VMEM((TOKENS, DB), BF16),
        pltpu.VMEM((512, DB), BF16), pltpu.VMEM((512, DB), BF16),
        pltpu.VMEM((512, DB), BF16), pltpu.VMEM((512, DB), BF16),
        pltpu.VMEM((512, DB), BF16), pltpu.VMEM((512, DB), BF16),
        pltpu.VMEM((5, 32, DB), BF16), pltpu.VMEM((5, 32, DB), BF16),
        pltpu.VMEM((3, COLS, DB), BF16), pltpu.VMEM((COLS, DB), F32), pltpu.VMEM((2, COLS, DB), F32),
        pltpu.VMEM((8, 16, 128), F32), pltpu.VMEM((8, 16, 128), F32), pltpu.VMEM((7, 16, 128), F32),
        pltpu.VMEM((16, 128), F32), pltpu.VMEM((16, 16, 128), F32),
        dma((5,)), dma, dma, dma((2,)), dma((2, 8)), dma((2, 5)),
        dma((2,)), dma((3, 5)), dma((2,)), dma((2, 5, 2)),
        dma((2,)), dma((2, 5)), dma((2, len(RING) // 2)), dma((2,)), dma, dma, dma((3,)), dma((3,)),
    ]
    held = pl.pallas_call(
        kernel,
        out_shape=[pltpu.VMEM(*x) for x in shapes],
        in_specs=[hbm] * 5,
        out_specs=[vm] * 5,
        scratch_shapes=scratch,
        compiler_params=pltpu.CompilerParams(
            collective_id=0, has_side_effects=True, vmem_limit_bytes=48 * 2**20
        ),
        cost_estimate=pl.CostEstimate(flops=6 * 2 * 1024 * 1024 * 896, bytes_accessed=12 * 2**20, transcendentals=0),
        name="block",
    )(field.reshape(COLS, DB), cotangent.reshape(COLS, DB), taps, w_in, w_out)
    result, fgrad, kgrad, grad_in, grad_out = pl.pallas_call(
        write_out,
        out_shape=[jax.ShapeDtypeStruct(*x) for x in shapes],
        in_specs=[hbm] * 5,
        out_specs=[pl.BlockSpec(memory_space=pltpu.HBM)] * 5,
        scratch_shapes=[dma((5,))],
        compiler_params=pltpu.CompilerParams(vmem_limit_bytes=2**20),
        name="write_out",
    )(*held)
    return (result.reshape(1, COLS, DB), fgrad.reshape(1, COLS, DB), grad_in, grad_out, kgrad)


def solution(mesh):
    space = P("space", None, "tensor")
    return jax.shard_map(
        on_device,
        mesh=mesh,
        in_specs=(space, P("tensor", "space"), P("space", "tensor"), P(None, "tensor"), space),
        out_specs=(space, space, P("tensor", "space"), P("space", "tensor"), P(None, "tensor")),
        check_vma=False,
    )
```
